32 devices in a mesh: dp: 4 (over y, x), tensor: 8 (over z, core).
Axes of the slice: x: 2, y: 2, z: 4, core: 2. Of those that a mesh axis runs over, the one named last changes fastest.
Arguments:
- tokens: bfloat16 [16384, 2048], P('dp'), may hold values from -6 to 6
- segment_ids: int32 [8, 2048], P('dp'), may hold values from 0 to 5, never falling along the last dimension, each value on 1 to 1024 neighbouring positions
- exit_layer: int32 [8, 2048], P('dp'), may hold values from 0 to 23
- norm1_gain: bfloat16 [2048], replicated, may hold values from 0.5 to 1.5
- norm1_shift: bfloat16 [2048], replicated, may hold values from -1.796875 to 1.796875
- w_qkv: bfloat16 [2048, 6144], P(None, 'tensor'), may hold values from -0.125 to 0.125
- b_qv: bfloat16 [4096], P('tensor'), may hold values from -3 to 3
- w_out: bfloat16 [2048, 2048], P('tensor'), may hold values from -0.5 to 0.5
- b_out: bfloat16 [2048], P('tensor'), may hold values from -3 to 3
- norm2_gain: bfloat16 [2048], replicated, may hold values from 0.15 to 4.5
- norm2_shift: bfloat16 [2048], replicated, may hold values from -1.796875 to 1.796875
- w_up: bfloat16 [2048, 8192], P(None, 'tensor'), may hold values from -0.125 to 0.125
- b_up: bfloat16 [8192], P('tensor'), may hold values from -3 to 3
- w_down: bfloat16 [8192, 2048], P('tensor'), may hold values from -0.0625 to 0.0625
- b_down: bfloat16 [2048], P('tensor'), may hold values from -3 to 3
- cotangent: bfloat16 [16384, 2048], P('dp', 'tensor'), may hold values from -6 to 6
Outputs:
- layer_output: bfloat16 [16384, 2048], P('dp', 'tensor')
- d_tokens: float32 [16384, 2048], P('dp', 'tensor')
- d_norm1_gain: float32 [2048], P('tensor')
- d_norm1_shift: float32 [2048], P('tensor')
- d_w_qkv: float32 [2048, 6144], P('dp', 'tensor')
- d_b_qv: float32 [4096], P('tensor')
- d_w_out: float32 [2048, 2048], P('tensor', 'dp')
- d_b_out: float32 [2048], P('tensor')
- d_norm2_gain: float32 [2048], P('tensor')
- d_norm2_shift: float32 [2048], P('tensor')
- d_w_up: float32 [2048, 8192], P('dp', 'tensor')
- d_b_up: float32 [8192], P('tensor')
- d_w_down: float32 [8192, 2048], P('tensor', 'dp')
- d_b_down: float32 [2048], P('tensor')
The draws below stay inside these ranges and needn't reach their ends.
Inputs may be any that keep to these rules, and one draw needn't show every extreme that they name: `segment_ids`: within a row the document numbers never fall; every number from 0 to 5 is used in each row, a document holds 1 to 1024 positions.
All inputs are finite; a program needn't handle non-finite values.
Results may differ from the reference program's by a relative error of at most 0.012.
Values may be sent and summed in bfloat16 or wider, within the bound.
No kernel may reach another device: no remote copies, remote signals or barrier semaphores. Data moves between devices by JAX's collectives and lax.ppermute only.
A program may use at most 320 MiB of HBM per device.

```python
import math
import jax
import jax.numpy as jnp
import numpy as np
from jax import lax

D = 2048
H = 32
HD = 64
FF = 8192
NLAYERS = 24
LAYER = 8
SEQ = 2048
DOCS = 6
ROWS = 8
TOKENS = 16384


def ramp_gain(key, ratio, lo, hi):
    place = jnp.arange(D, dtype=jnp.float32) / max(D - 1, 1)
    ramp = jnp.exp(math.log(ratio) * (place - 0.5))
    factor = jax.random.uniform(key, (D,), jnp.float32, lo, hi)
    return ramp * factor


def draw_norm2_gain(key, part):
    key = jax.random.fold_in(key, 7)
    values = ramp_gain(key, 4.0, 0.7, 1.3)
    return values.astype(jnp.bfloat16)


def touch_ends(result, key, least, top_value):
    extent = result.shape
    spot = [jax.random.randint(jax.random.fold_in(key, axis), (), 0, extent[axis]) for axis in range(len(extent))]
    result = result.at[tuple(spot)].set(least)
    longest = extent.index(max(extent))
    spot[longest] = (spot[longest] + 1) % extent[longest]
    return result.at[tuple(spot)].set(top_value)


def block_scale(rng, shape, split, smallest, high):
    factor_of = 1.0
    for axis_at, parts in split:
        heights = jax.random.uniform(jax.random.fold_in(jax.random.fold_in(rng, 6), axis_at), (parts,), jnp.float32, smallest / len(split), high / len(split))
        factor_of = factor_of * jnp.repeat(jnp.exp(heights), shape[axis_at] // parts).reshape((-1,) + (1,) * (len(shape) - 1 - axis_at))
    return factor_of


def split_up(number_of, total, most, lean):
    portions = [(1 << 20) // math.isqrt(rank ** lean) + 1 for rank in range(2, number_of + 1)]
    spare, holding = total - most - (number_of - 1), [1] * (number_of - 1)
    while spare > 0:
        movable = [i for i in range(number_of - 1) if holding[i] < most]
        mass, left = sum([portions[i] for i in movable]), spare
        for i in movable:
            more = min(most - holding[i], max(1, left * portions[i] // mass), spare)
            holding[i] = holding[i] + more
            spare = spare - more
    return np.array([most] + holding)


def ragged(own_key, number_of, total, bound, slope):
    if number_of == 2:
        one = jax.random.randint(own_key, (), max(1, total - bound), min(bound, total - 1) + 1)
        return jnp.stack([one, total - one])
    sizes = jnp.asarray(split_up(number_of, total, bound, slope), jnp.int32)
    twos = (number_of - 1) // 2
    donor, sink = sizes[1:1 + 2 * twos:2], sizes[2:2 + 2 * twos:2]
    slack = jnp.minimum(donor - 1, bound - sink)
    shifted = jax.random.randint(jax.random.fold_in(own_key, 1), (twos,), 0, 1 << 20) % (slack + 1)
    sizes = sizes.at[1:1 + 2 * twos:2].set(donor - shifted).at[2:2 + 2 * twos:2].set(sink + shifted)
    return sizes[jax.random.permutation(jax.random.fold_in(own_key, 2), number_of)]


def noise(own_key, shape, scale, bound, split=(), kind=jnp.bfloat16):
    array = scale * jax.random.normal(own_key, shape, jnp.float32)
    if split:
        array = array * block_scale(own_key, shape, split, -0.22, 0.18)
    return jnp.clip(array, -bound, bound).astype(kind)


def setup_inputs(seed: int = 0) -> dict:
    arg_keys = jax.random.split(jax.random.key(seed), 17)
    tokens = noise(arg_keys[0], (TOKENS, D), 1.0, 6.0, ((0, 4),))
    segment_ids = jax.vmap(lambda own: jnp.searchsorted(jnp.cumsum(ragged(own, DOCS, SEQ, SEQ // 2, 2)), jnp.arange(SEQ), side="right"))(jax.random.split(arg_keys[1], ROWS)).reshape((ROWS, SEQ)).astype(jnp.int32)
    exit_layer = touch_ends(jax.random.randint(arg_keys[2], (ROWS, SEQ), 0, NLAYERS), jax.random.fold_in(arg_keys[2], 1), 0, NLAYERS - 1).astype(jnp.int32)
    norm1_gain = jnp.clip(1.0 + 0.1 * jax.random.normal(arg_keys[3], (D,), jnp.float32), 0.5, 1.5).astype(jnp.bfloat16)
    norm1_shift = noise(arg_keys[4], (D,), 0.3, 1.796875)
    w_qkv = noise(arg_keys[5], (D, 3 * H * HD), D ** -0.5, 0.125, ((1, 8),))
    b_qv = noise(arg_keys[6], (2 * H * HD,), 0.5, 3.0, ((0, 8),))
    w_out = noise(arg_keys[7], (H * HD, D), (H * HD // 16) ** -0.5, 0.5, ((0, 8),))
    b_out = noise(arg_keys[8], (D,), 0.5, 3.0, ((0, 8),))
    norm2_gain = draw_norm2_gain(jax.random.fold_in(arg_keys[16], 71), 0)
    norm2_shift = noise(arg_keys[10], (D,), 0.3, 1.796875)
    w_up = noise(arg_keys[11], (D, FF), D ** -0.5, 0.125, ((1, 8),))
    b_up = noise(arg_keys[12], (FF,), 0.5, 3.0, ((0, 8),))
    w_down = noise(arg_keys[13], (FF, D), FF ** -0.5, 0.0625, ((0, 8),))
    b_down = noise(arg_keys[14], (D,), 0.5, 3.0, ((0, 8),))
    cotangent = noise(arg_keys[15], (TOKENS, D), 1.0, 6.0, ((0, 4), (1, 8)))
    return dict(tokens=tokens, segment_ids=segment_ids, exit_layer=exit_layer, norm1_gain=norm1_gain, norm1_shift=norm1_shift, w_qkv=w_qkv, b_qv=b_qv, w_out=w_out, b_out=b_out, norm2_gain=norm2_gain, norm2_shift=norm2_shift, w_up=w_up, b_up=b_up, w_down=w_down, b_down=b_down, cotangent=cotangent)


EPSILON = 1e-05
MASKED = -1e+30
HIGHEST = lax.Precision.HIGHEST

@jax.custom_vjp
def low(v):
    return lax.optimization_barrier(v.astype(jnp.bfloat16)).astype(jnp.float32)

@jax.custom_vjp
def low_back(v):
    return v

def low_keep(v):
    return (low(v), None)

def low_pass(kept, grad):
    return (grad,)

def back_keep(v):
    return (v, None)

def back_low(kept, grad):
    return (low(grad),)
low.defvjp(low_keep, low_pass)
low_back.defvjp(back_keep, back_low)

def layer_norm(values, gain, shift):
    centre = lax.optimization_barrier(jnp.mean(values, axis=-1, keepdims=True))
    spread = lax.optimization_barrier(jnp.mean(jnp.square(values - centre), axis=-1, keepdims=True))
    return (values - centre) * lax.rsqrt(spread + EPSILON) * gain + shift

def visible(row_docs, block_start, block_rows):
    docs_query = lax.dynamic_slice_in_dim(row_docs, block_start, block_rows)
    pos_query = block_start + jnp.arange(block_rows, dtype=jnp.int32)
    pos_key = jnp.arange(row_docs.shape[0], dtype=jnp.int32)
    return (pos_key[None, :] <= pos_query[:, None]) & (row_docs[None, :] == docs_query[:, None])

def attend_block(block_start, queries, key_rows, value_rows, row_docs):
    block_rows = min(512, SEQ)
    query_block = lax.dynamic_slice_in_dim(queries, block_start, block_rows, 1)
    scores = jnp.einsum('hqe,hke->hqk', query_block, key_rows, precision=HIGHEST) * HD ** (-0.5)
    scores = jnp.where(visible(row_docs, block_start, block_rows)[None], low_back(scores), MASKED)
    row_top = lax.optimization_barrier(jnp.max(scores, axis=-1, keepdims=True))
    weights = jnp.exp(scores - row_top)
    shares = weights / lax.optimization_barrier(jnp.sum(weights, axis=-1, keepdims=True))
    return jnp.einsum('hqk,hke->hqe', low(shares), value_rows, precision=HIGHEST)

def run_row(row_values, row_docs, row_active, weights):
    gain1, shift1, w_qkv, b_qv, w_out, b_out, gain2, shift2, w_up, b_up, w_down, b_down = weights
    block_rows = min(512, SEQ)
    normed1 = low(layer_norm(row_values, gain1, shift1))
    packed = jnp.dot(normed1, w_qkv, precision=HIGHEST).reshape(SEQ, H, 3, HD)
    biases = b_qv.reshape(H, 2, HD)
    queries = low_back(low(packed[:, :, 0] + biases[:, 0])).transpose(1, 0, 2)
    key_rows = low_back(low(packed[:, :, 1])).transpose(1, 0, 2)
    value_rows = low_back(low(packed[:, :, 2] + biases[:, 1])).transpose(1, 0, 2)
    block_fn = jax.checkpoint(attend_block)
    starts = jnp.arange(SEQ // block_rows, dtype=jnp.int32) * block_rows
    mixed = lax.map(lambda block_start: block_fn(block_start, queries, key_rows, value_rows, row_docs), starts)
    head_out = low_back(low(mixed.transpose(0, 2, 1, 3).reshape(SEQ, H * HD)))
    branch = low_back(jnp.dot(head_out, w_out, precision=HIGHEST) + b_out)
    residual = row_values + row_active[:, None] * branch
    normed2 = low(layer_norm(residual, gain2, shift2))
    hidden = low_back(jnp.dot(normed2, w_up, precision=HIGHEST) + b_up)
    activated = low(jax.nn.gelu(hidden, approximate=True))
    return residual + row_active[:, None] * (jnp.dot(activated, w_down, precision=HIGHEST) + b_down)

def reference(tokens, segment_ids, exit_layer, norm1_gain, norm1_shift, w_qkv, b_qv, w_out, b_out, norm2_gain, norm2_shift, w_up, b_up, w_down, b_down, cotangent):
    weights = tuple((item.astype(jnp.float32) for item in (norm1_gain, norm1_shift, w_qkv, b_qv, w_out, b_out, norm2_gain, norm2_shift, w_up, b_up, w_down, b_down)))
    row_inputs = tokens.astype(jnp.float32).reshape(ROWS, SEQ, D)
    active = (exit_layer > LAYER).astype(jnp.float32)
    row_fn = jax.checkpoint(run_row)

    def forward(row_inputs, weights):

        def scan_step(carried, row_item):
            return (carried, row_fn(row_item[0], row_item[1], row_item[2], weights))
        _, outputs = lax.scan(scan_step, jnp.float32(0.0), (row_inputs, segment_ids, active))
        return outputs
    outputs, pullback = jax.vjp(forward, row_inputs, weights)
    d_rows, d_weights = pullback(cotangent.astype(jnp.float32).reshape(ROWS, SEQ, D))
    return (outputs.reshape(TOKENS, D).astype(jnp.bfloat16), d_rows.reshape(TOKENS, D), d_weights[0], d_weights[1], d_weights[2], d_weights[3], d_weights[4], d_weights[5], d_weights[6], d_weights[7], d_weights[8], d_weights[9], d_weights[10], d_weights[11])
```

```python
import functools

import jax
import jax.numpy as jnp
from jax import lax
from jax.experimental import pallas as pl
from jax.experimental.pallas import tpu as pltpu
from jax.sharding import Mesh, PartitionSpec as P

HD = 64
LAYER = 8
DOCS = 6
EPSILON = 1e-05
MASKED = -1e30
SCALE = HD ** (-0.5)
F32 = jnp.float32
BF = jnp.bfloat16

BQ = 256
BK = 512

NT = (((1,), (1,)), ((), ()))
TN = (((0,), (0,)), ((), ()))


def mm(left, right):
    return jnp.dot(left, right, preferred_element_type=F32)


def mm_nt(left, right):
    return lax.dot_general(left, right, NT, preferred_element_type=F32)


def mm_tn(left, right):
    return lax.dot_general(left, right, TN, preferred_element_type=F32)


def split_heads(pairs, heads):
    lane = lax.broadcasted_iota(jnp.int32, (pairs.shape[0], 128), 1)
    out = []
    for pair in range(heads // 2):
        part = pairs[:, 128 * pair : 128 * pair + 128]
        zero = jnp.zeros_like(part)
        out += [jnp.where(lane < 64, part, zero), jnp.where(lane < 64, zero, part)]
    return out


def merge_heads(parts, block):
    row = lax.broadcasted_iota(jnp.int32, (128, block), 0)
    return [
        jnp.where(row < 64, parts[2 * pair], parts[2 * pair + 1])
        for pair in range(len(parts) // 2)
    ]


def attend_kernel(
    heads, first, last, q_ref, k_ref, v_ref, lo_ref, hi_ref, o_ref, low_ref, lse_ref
):
    block = pl.program_id(0)
    queries = split_heads(q_ref[...] * jnp.asarray(SCALE, BF), heads)
    lo = lo_ref[...]
    hi = hi_ref[...]

    def step(key_block, carried):
        start = pl.multiple_of(key_block * BK, BK)
        key_pos = start + lax.broadcasted_iota(jnp.int32, (BK, BQ), 0)
        allowed = (key_pos >= lo) & (key_pos <= hi)
        raw = [
            mm_nt(k_ref[pl.ds(start, BK), 128 * (h // 2) : 128 * (h // 2) + 128], queries[h])
            for h in range(heads)
        ]
        out = []
        for h in range(heads):
            values = v_ref[pl.ds(start, BK), 128 * (h // 2) : 128 * (h // 2) + 128]
            top, total, mixed = carried[3 * h : 3 * h + 3]
            scores = jnp.where(allowed, raw[h], MASKED)
            new_top = jnp.maximum(top, jnp.max(scores, axis=0, keepdims=True))
            weights = jnp.exp(scores - new_top)
            fade = jnp.exp(top - new_top)
            total = total * fade + jnp.sum(weights, axis=0, keepdims=True)
            mixed = mixed * fade + mm_tn(values, weights.astype(BF))
            out += [new_top, total, mixed]
        return tuple(out)

    init = (
        jnp.full((1, BQ), MASKED, F32),
        jnp.zeros((1, BQ), F32),
        jnp.zeros((128, BQ), F32),
    ) * heads
    done = lax.fori_loop(first[block], last[block], step, init)
    merged = merge_heads([done[3 * h + 2] / done[3 * h + 1] for h in range(heads)], BQ)
    for pair in range(heads // 2):
        part = merged[pair].T
        o_ref[:, 128 * pair : 128 * pair + 128] = part
        low_ref[:, 128 * pair : 128 * pair + 128] = part.astype(BF)
    row = lax.broadcasted_iota(jnp.int32, (8, BQ), 0)
    lse = jnp.zeros((8, BQ), F32)
    for h in range(heads):
        lse = jnp.where(row == h, done[3 * h] + jnp.log(done[3 * h + 1]), lse)
    lse_ref[...] = lse


def attend(queries, packed, lo, hi, first, last):
    count, width = queries.shape
    length = packed.shape[0]
    heads = width // HD
    row_spec = pl.BlockSpec((1, BQ), lambda i, *_: (0, i))
    block_spec = pl.BlockSpec((BQ, width), lambda i, *_: (i, 0))
    spec = pltpu.PrefetchScalarGridSpec(
        num_scalar_prefetch=2,
        grid=(count // BQ,),
        in_specs=[
            block_spec,
            pl.BlockSpec((length, width), lambda i, *_: (0, 1)),
            pl.BlockSpec((length, width), lambda i, *_: (0, 2)),
            row_spec,
            row_spec,
        ],
        out_specs=[block_spec, block_spec, pl.BlockSpec((8, BQ), lambda i, *_: (0, i))],
    )
    return pl.pallas_call(
        functools.partial(attend_kernel, heads),
        grid_spec=spec,
        out_shape=[
            jax.ShapeDtypeStruct((count, width), F32),
            jax.ShapeDtypeStruct((count, width), BF),
            jax.ShapeDtypeStruct((8, count), F32),
        ],
        compiler_params=pltpu.CompilerParams(vmem_limit_bytes=48 * 2**20),
        cost_estimate=pl.CostEstimate(
            flops=6 * count * length * width, bytes_accessed=8 * count * width, transcendentals=0
        ),
        name="attend",
    )(first, last, queries, packed, packed, lo, hi)


def attend_back_kernel(
    heads,
    first,
    last,
    q_ref,
    k_ref,
    v_ref,
    g_ref,
    o_ref,
    lse_ref,
    lo_ref,
    hi_ref,
    dq_ref,
    dk_ref,
    dv_ref,
    dk_sum,
    dv_sum,
):
    count, width = q_ref.shape
    dk_sum[...] = jnp.zeros_like(dk_sum)
    dv_sum[...] = jnp.zeros_like(dv_sum)
    head_of = lax.broadcasted_iota(jnp.int32, (8, width), 1) // HD
    picks = (head_of == lax.broadcasted_iota(jnp.int32, (8, width), 0)).astype(F32)

    def query_step(block, _):
        at = pl.multiple_of(block * BQ, BQ)
        queries = split_heads(q_ref[pl.ds(at, BQ), :] * jnp.asarray(SCALE, BF), heads)
        grad = g_ref[pl.ds(at, BQ), :]
        grads = split_heads(grad, heads)
        lo = lo_ref[:, pl.ds(at, BQ)]
        hi = hi_ref[:, pl.ds(at, BQ)]
        delta = lax.dot_general(
            picks,
            grad.astype(F32) * o_ref[pl.ds(at, BQ), :],
            NT,
            precision=lax.Precision.HIGHEST,
            preferred_element_type=F32,
        )

        def key_step(key_block, carried):
            start = pl.multiple_of(key_block * BK, BK)
            key_pos = start + lax.broadcasted_iota(jnp.int32, (BK, BQ), 0)
            allowed = (key_pos >= lo) & (key_pos <= hi)
            out = []
            for pair in range(heads // 2):
                lanes = slice(128 * pair, 128 * pair + 128)
                keys = k_ref[pl.ds(start, BK), lanes]
                values = v_ref[pl.ds(start, BK), lanes]
                dk = dk_sum[pl.ds(start, BK), lanes]
                dv = dv_sum[pl.ds(start, BK), lanes]
                for h in (2 * pair, 2 * pair + 1):
                    scores = mm_nt(keys, queries[h])
                    shares = jnp.exp(
                        jnp.where(allowed, scores, MASKED) - lse_ref[h : h + 1, pl.ds(at, BQ)]
                    )
                    d_shares = mm_nt(values, grads[h])
                    d_scores = (shares * (d_shares - delta[h : h + 1, :])).astype(BF)
                    dv = dv + mm(shares.astype(BF), grads[h])
                    dk = dk + mm(d_scores, queries[h])
                    out.append(carried[h] + mm_tn(keys, d_scores))
                dk_sum[pl.ds(start, BK), lanes] = dk
                dv_sum[pl.ds(start, BK), lanes] = dv
            return tuple(out)

        done = lax.fori_loop(
            first[block], last[block], key_step, (jnp.zeros((128, BQ), F32),) * heads
        )
        merged = merge_heads(done, BQ)
        for pair in range(heads // 2):
            dq_ref[pl.ds(at, BQ), 128 * pair : 128 * pair + 128] = (merged[pair].T * SCALE).astype(
                BF
            )
        return 0

    lax.fori_loop(0, count // BQ, query_step, 0)
    dk_ref[...] = dk_sum[...].astype(BF)
    dv_ref[...] = dv_sum[...].astype(BF)


def attend_back(queries, packed, grad, mixed, lse, lo, hi, first, last):
    count, width = queries.shape
    length = packed.shape[0]
    heads = width // HD
    query_spec = pl.BlockSpec((count, width), lambda i, *_: (0, 0))
    key_spec = pl.BlockSpec((length, width), lambda i, *_: (0, 0))
    row_spec = pl.BlockSpec((1, count), lambda i, *_: (0, 0))
    spec = pltpu.PrefetchScalarGridSpec(
        num_scalar_prefetch=2,
        grid=(1,),
        in_specs=[
            query_spec,
            pl.BlockSpec((length, width), lambda i, *_: (0, 1)),
            pl.BlockSpec((length, width), lambda i, *_: (0, 2)),
            query_spec,
            query_spec,
            pl.BlockSpec((8, count), lambda i, *_: (0, 0)),
            row_spec,
            row_spec,
        ],
        out_specs=[query_spec, key_spec, key_spec],
        scratch_shapes=[pltpu.VMEM((length, width), F32), pltpu.VMEM((length, width), F32)],
    )
    return pl.pallas_call(
        functools.partial(attend_back_kernel, heads),
        grid_spec=spec,
        out_shape=[
            jax.ShapeDtypeStruct((count, width), BF),
            jax.ShapeDtypeStruct((length, width), BF),
            jax.ShapeDtypeStruct((length, width), BF),
        ],
        compiler_params=pltpu.CompilerParams(vmem_limit_bytes=56 * 2**20),
        cost_estimate=pl.CostEstimate(
            flops=10 * count * length * width, bytes_accessed=8 * count * width, transcendentals=0
        ),
        name="attend_back",
    )(first, last, queries, packed, packed, grad, mixed, lse, lo, hi)


def running_count(flags):
    rows, length = flags.shape
    chunk = 128
    tiles = flags.reshape(rows, length // chunk, chunk)
    ones = (
        lax.broadcasted_iota(jnp.int32, (chunk, chunk), 0)
        <= lax.broadcasted_iota(jnp.int32, (chunk, chunk), 1)
    ).astype(BF)
    inside = jnp.einsum("rtc,cd->rtd", tiles.astype(BF), ones, preferred_element_type=F32)
    totals = jnp.sum(tiles, axis=2)
    tile_count = length // chunk
    earlier = (
        lax.broadcasted_iota(jnp.int32, (tile_count, tile_count), 0)
        < lax.broadcasted_iota(jnp.int32, (tile_count, tile_count), 1)
    ).astype(F32)
    before = jnp.sum(totals[:, :, None] * earlier[None], axis=1)
    return (inside + before[:, :, None]).reshape(rows, length)


def swap_halves(value):
    return lax.ppermute(value, "half", [(0, 1), (1, 0)])


def fetch_other(weight):
    part = weight.shape[0] // lax.axis_size("dp")
    own = lax.dynamic_slice_in_dim(weight, lax.axis_index("dp") * part, part, 0)
    return lax.all_gather(swap_halves(own), "dp", axis=0, tiled=True)


def sum_over_dp(grad, dimension):
    return lax.psum_scatter(grad, "dp", scatter_dimension=dimension, tiled=True)


ALL = ("half", "tp")


def layer(
    capacity,
    tokens,
    segment_ids,
    exit_layer,
    norm1_gain,
    norm1_shift,
    w_qkv,
    b_qv,
    w_out,
    b_out,
    norm2_gain,
    norm2_shift,
    w_up,
    b_up,
    w_down,
    b_down,
    cotangent,
):
    n_tp = lax.axis_size("tp")
    half = lax.axis_index("half")
    place = lax.axis_index("tp")
    rows, length = segment_ids.shape
    width = tokens.shape[1]
    own_width = cotangent.shape[1]
    device = half * n_tp + place
    own_heads = b_qv.shape[0] // (2 * HD)
    cap_all = -(-capacity // BQ) * BQ
    cap_part = capacity // n_tp
    part = length // n_tp

    active = exit_layer > LAYER
    running = running_count(active.astype(F32)).astype(jnp.int32)
    slot = jnp.where(active, running - 1, -1)
    slots = lax.broadcasted_iota(jnp.int32, (1, cap_all, 1), 1)
    picks = (slots == slot[:, None, :]).astype(BF)
    own_pick = lax.dynamic_index_in_dim(picks, half, 0, keepdims=False)
    own_slot = lax.dynamic_index_in_dim(slot, half, 0, keepdims=False)
    own_count = lax.dynamic_index_in_dim(running[:, -1], half, 0, keepdims=False)
    own_docs = lax.dynamic_index_in_dim(segment_ids, half, 0, keepdims=False)
    doc_numbers = jnp.arange(DOCS, dtype=jnp.int32)[:, None]
    doc_starts = jnp.sum((own_docs[None, :] < doc_numbers).astype(jnp.int32), axis=1, keepdims=True)
    starts = jnp.sum(jnp.where(own_docs[None, :] == doc_numbers, doc_starts, 0), axis=0)
    position = lax.broadcasted_iota(jnp.int32, (1, length), 1)
    chosen = slots[0] == own_slot[None, :]
    filled = jnp.arange(cap_all, dtype=jnp.int32) < own_count
    hi = jnp.where(filled, jnp.sum(jnp.where(chosen, position, 0), axis=1), length - 1)
    lo = jnp.where(filled, jnp.sum(jnp.where(chosen, starts[None, :], 0), axis=1), starts[-1])
    first = lo[::BQ] // BK
    last = hi[BQ - 1 :: BQ] // BK + 1
    lo = lo[None]
    hi = hi[None]

    def by_kind(weight):
        return weight.reshape(width, own_heads, 3, HD).swapaxes(1, 2).reshape(width, -1)

    def qkv_bias(bias):
        pairs = bias.astype(F32).reshape(own_heads, 2, HD)
        return jnp.concatenate(
            (
                pairs[:, 0].reshape(-1),
                jnp.zeros((own_heads * HD,), F32),
                pairs[:, 1].reshape(-1),
            )
        )

    own_qkv = by_kind(w_qkv)
    far_qkv = fetch_other(own_qkv)
    far_out = fetch_other(w_out)
    far_up = fetch_other(w_up)
    far_down = fetch_other(w_down)
    far_bias = swap_halves(jnp.concatenate((b_qv, b_up)))
    far_b_qv, far_b_up = far_bias[: b_qv.shape[0]], far_bias[b_qv.shape[0] :]
    out_biases = lax.all_gather(jnp.stack((b_out, b_down)), ALL, axis=1, tiled=True).astype(F32)

    own_cot = jnp.einsum(
        "rcp,rpf->rcf",
        picks[:, :capacity],
        cotangent.reshape(rows, length, own_width),
        preferred_element_type=F32,
    ).astype(BF)
    cot = lax.all_to_all(
        own_cot.reshape(rows * capacity, own_width), ALL, split_axis=0, concat_axis=1, tiled=True
    )
    d_ffn = lax.all_gather(cot, "tp", axis=0, tiled=True)

    inputs = lax.dynamic_slice_in_dim(tokens, half * length, length, 0)
    wide = inputs.astype(F32)
    mean1 = jnp.mean(wide, axis=1, keepdims=True)
    inv1 = lax.rsqrt(jnp.mean(jnp.square(wide - mean1), axis=1, keepdims=True) + EPSILON)
    gain1 = norm1_gain.astype(F32)
    normed1 = ((wide - mean1) * inv1 * gain1 + norm1_shift.astype(F32)).astype(BF)

    if own_heads % 2:
        far_first = own_heads * HD
        sets = [
            (
                jnp.concatenate(
                    (
                        own_qkv.reshape(width, 3, far_first),
                        far_qkv.reshape(width, 3, far_first),
                    ),
                    axis=2,
                ).reshape(width, -1),
                jnp.concatenate(
                    (
                        qkv_bias(b_qv).reshape(3, far_first),
                        qkv_bias(far_b_qv).reshape(3, far_first),
                    ),
                    axis=1,
                ).reshape(-1),
            )
        ]
    else:
        sets = [(own_qkv, qkv_bias(b_qv)), (far_qkv, qkv_bias(far_b_qv))]

    kept = []
    for weight, bias in sets:
        packed = (mm(normed1, weight) + bias).astype(BF)
        head_width = packed.shape[1] // 3
        queries = mm(own_pick, packed[:, :head_width]).astype(BF)
        mixed, mixed_low, lse = attend(queries, packed, lo, hi, first, last)
        kept.append((packed, queries, mixed, mixed_low, lse))
    head_out = jnp.concatenate([item[3] for item in kept], axis=1)[:capacity]
    out_weight = jnp.concatenate((w_out, far_out), axis=0)
    branch = lax.psum_scatter(
        mm(head_out, out_weight).astype(BF), "tp", scatter_dimension=0, tiled=True
    ).astype(F32)

    part_pick = lax.dynamic_slice_in_dim(own_pick, place * cap_part, cap_part, 0)
    residual = mm(part_pick, inputs) + branch + out_biases[0]
    mean2 = jnp.mean(residual, axis=1, keepdims=True)
    inv2 = lax.rsqrt(jnp.mean(jnp.square(residual - mean2), axis=1, keepdims=True) + EPSILON)
    standard2 = (residual - mean2) * inv2
    gain2 = norm2_gain.astype(F32)
    normed2 = lax.all_gather(
        (standard2 * gain2 + norm2_shift.astype(F32)).astype(BF), "tp", axis=0, tiled=True
    )

    up_weights = (w_up, far_up)
    down_weights = (w_down, far_down)
    acts = []
    d_hiddens = []
    for up, down, bias in zip(up_weights, down_weights, (b_up, far_b_up)):
        hidden = mm(normed2, up) + bias.astype(F32)
        activated, gelu_back = jax.vjp(lambda u: jax.nn.gelu(u, approximate=True), hidden)
        acts.append(activated.astype(BF))
        d_hiddens.append(gelu_back(mm_nt(d_ffn, down))[0].astype(BF))
    d_normed2 = lax.psum_scatter(
        (mm_nt(d_hiddens[0], w_up) + mm_nt(d_hiddens[1], far_up)).astype(BF),
        "tp",
        scatter_dimension=0,
        tiled=True,
    ).astype(F32)
    ffn_out = lax.psum_scatter(
        (mm(acts[0], w_down) + mm(acts[1], far_down)).astype(BF),
        "tp",
        scatter_dimension=0,
        tiled=True,
    ).astype(F32)
    out_part = (residual + ffn_out + out_biases[1]).astype(BF)
    out_slots = lax.all_to_all(out_part, ALL, split_axis=1, concat_axis=0, tiled=True)

    def to_tokens(slot_values):
        return jnp.einsum(
            "rcp,rcf->rpf",
            picks[:, :capacity],
            slot_values.reshape(rows, capacity, own_width),
            preferred_element_type=F32,
        ).reshape(rows * length, own_width)

    active_column = active.reshape(rows * length, 1)
    own_tokens = lax.dynamic_slice_in_dim(tokens, device * own_width, own_width, 1)
    result = jnp.where(active_column, to_tokens(out_slots).astype(BF), own_tokens)

    g2 = d_normed2 * gain2
    d_residual = cot.astype(F32) + inv2 * (
        g2
        - jnp.mean(g2, axis=1, keepdims=True)
        - standard2 * jnp.mean(g2 * standard2, axis=1, keepdims=True)
    )
    d_branch_part = d_residual.astype(BF)
    d_branch = lax.all_gather(d_branch_part, "tp", axis=0, tiled=True)
    d_residual_slots = lax.all_to_all(
        d_branch_part, ALL, split_axis=1, concat_axis=0, tiled=True
    )
    d_heads = mm_nt(d_branch, out_weight).astype(BF)
    d_heads = jnp.pad(d_heads, ((0, cap_all - capacity), (0, 0)))

    d_packs = []
    at = 0
    for packed, queries, mixed, _, lse in kept:
        head_width = queries.shape[1]
        grad = d_heads[:, at : at + head_width]
        at += head_width
        dq, dk, dv = attend_back(queries, packed, grad, mixed, lse, lo, hi, first, last)
        dq = mm_tn(own_pick, dq).astype(BF)
        d_packs.append(jnp.concatenate((dq, dk, dv), axis=1))
    d_normed1 = lax.psum_scatter(
        sum(mm_nt(grad, item[0]) for grad, item in zip(d_packs, sets)).astype(BF),
        "tp",
        scatter_dimension=0,
        tiled=True,
    ).astype(F32)

    def own_part(value):
        return lax.dynamic_slice_in_dim(value, place * part, part, 0)

    standard1 = (own_part(inputs).astype(F32) - own_part(mean1)) * own_part(inv1)
    g1 = d_normed1 * gain1
    d_norm1 = own_part(inv1) * (
        g1
        - jnp.mean(g1, axis=1, keepdims=True)
        - standard1 * jnp.mean(g1 * standard1, axis=1, keepdims=True)
    )
    d_norm1_tokens = lax.all_to_all(
        d_norm1.astype(BF), ALL, split_axis=1, concat_axis=0, tiled=True
    )
    d_inputs = d_norm1_tokens.astype(F32) + jnp.where(
        active_column, to_tokens(d_residual_slots), cotangent.astype(F32)
    )

    def split_far(grad, dimension):
        if len(d_packs) == 2:
            return grad
        size = grad.shape[dimension] // 2
        return [
            lax.slice_in_dim(grad, 0, size, axis=dimension),
            lax.slice_in_dim(grad, size, 2 * size, axis=dimension),
        ]

    def reduce_pair(own, far, dimension):
        far_sum = sum_over_dp(far.astype(BF), dimension)
        own_sum = sum_over_dp(own.astype(BF), dimension)
        return own_sum.astype(F32) + swap_halves(far_sum).astype(F32)

    if len(d_packs) == 1:
        pack = d_packs[0].reshape(length, 3, 2, own_heads * HD)
        d_packs = [pack[:, :, i].reshape(length, -1) for i in range(2)]
    grad_down = reduce_pair(mm_tn(acts[0], d_ffn), mm_tn(acts[1], d_ffn), 1)
    grad_up = reduce_pair(mm_tn(normed2, d_hiddens[0]), mm_tn(normed2, d_hiddens[1]), 0)
    own_out = own_heads * HD
    grad_out = reduce_pair(
        mm_tn(head_out[:, :own_out], d_branch), mm_tn(head_out[:, own_out:], d_branch), 1
    )
    grad_qkv = reduce_pair(mm_tn(normed1, d_packs[0]), mm_tn(normed1, d_packs[1]), 0)
    grad_qkv = (
        grad_qkv.reshape(-1, 3, own_heads, HD).swapaxes(1, 2).reshape(-1, 3 * own_heads * HD)
    )

    def bias_sums(pack, d_hidden):
        sums = jnp.sum(pack.astype(F32), axis=0).reshape(3, own_heads, HD)
        return jnp.concatenate(
            (
                jnp.stack((sums[0], sums[2]), axis=1).reshape(-1),
                jnp.sum(d_hidden.astype(F32), axis=0),
            )
        )

    unit_sums = bias_sums(d_packs[0], d_hiddens[0]) + swap_halves(
        bias_sums(d_packs[1], d_hiddens[1])
    )
    features = jnp.stack(
        (
            jnp.sum(d_normed1 * standard1, axis=0),
            jnp.sum(d_normed1, axis=0),
            jnp.sum(d_normed2 * standard2, axis=0),
            jnp.sum(d_normed2, axis=0),
            jnp.sum(d_branch_part.astype(F32), axis=0),
            jnp.sum(cot.astype(F32), axis=0),
        )
    )
    spread = lax.all_to_all(features, ALL, split_axis=1, concat_axis=0, tiled=True)
    feature_sums = jnp.sum(spread.reshape(-1, 6, own_width), axis=0).reshape(-1)
    summed = lax.psum(jnp.concatenate((feature_sums, unit_sums)), "dp")
    feature_sums = summed[: 6 * own_width].reshape(6, own_width)
    unit_sums = summed[6 * own_width :]
    size = b_qv.shape[0]
    return (
        result,
        d_inputs,
        feature_sums[0],
        feature_sums[1],
        grad_qkv,
        unit_sums[:size],
        grad_out,
        feature_sums[4],
        feature_sums[2],
        feature_sums[3],
        grad_up,
        unit_sums[size:],
        grad_down,
        feature_sums[5],
    )


def per_device(*args):
    exit_layer = args[2]
    length = exit_layer.shape[1]
    small = length * 11 // 16
    counts = jnp.sum((exit_layer > LAYER).astype(F32), axis=1)
    most = lax.pmax(jnp.max(counts), "dp")
    return lax.cond(
        most <= small,
        functools.partial(layer, small),
        functools.partial(layer, length),
        *args,
    )


def solution(mesh):
    split = Mesh(mesh.devices.reshape(mesh.shape["dp"], 2, -1), ("dp", "half", "tp"))
    tensor = ("half", "tp")
    return jax.shard_map(
        per_device,
        mesh=split,
        in_specs=(
            P("dp", None),
            P("dp", None),
            P("dp", None),
            P(),
            P(),
            P(None, tensor),
            P(tensor),
            P(tensor, None),
            P(tensor),
            P(),
            P(),
            P(None, tensor),
            P(tensor),
            P(tensor, None),
            P(tensor),
            P("dp", tensor),
        ),
        out_specs=(
            P("dp", tensor),
            P("dp", tensor),
            P(tensor),
            P(tensor),
            P("dp", tensor),
            P(tensor),
            P(tensor, "dp"),
            P(tensor),
            P(tensor),
            P(tensor),
            P("dp", tensor),
            P(tensor),
            P(tensor, "dp"),
            P(tensor),
        ),
        check_vma=False,
    )
```

```python
import functools

import jax
import jax.numpy as jnp
from jax import lax
from jax.experimental import pallas as pl
from jax.experimental.pallas import tpu as pltpu
from jax.sharding import Mesh, PartitionSpec as P

HD = 64
LAYER = 8
DOCS = 6
EPSILON = 1e-05
MASKED = -1e30
SCALE = HD ** (-0.5)
F32 = jnp.float32
BF = jnp.bfloat16

BQ = 256
BK = 512

BRIEF = pl.CostEstimate(flops=1, bytes_accessed=1, transcendentals=0)

NT = (((1,), (1,)), ((), ()))
TN = (((0,), (0,)), ((), ()))


def mm(left, right):
    return jnp.dot(left, right, preferred_element_type=F32)


def mm_nt(left, right):
    return lax.dot_general(left, right, NT, preferred_element_type=F32)


def mm_tn(left, right):
    return lax.dot_general(left, right, TN, preferred_element_type=F32)


def tie(value, *others):
    return lax.optimization_barrier((value, *others))[0]


def matmul_kernel(dims, at, left_ref, right_ref, *refs):
    out = lax.dot_general(left_ref[...], right_ref[...], dims, preferred_element_type=F32)
    if len(refs) == 2:
        out = out + refs[0][...]
    refs[-1][...] = out.astype(BF)


def brief_mm(left, right, bias=None, transposed=False, half=None):
    rows, depth = left.shape
    at = jnp.zeros((1,), jnp.int32) if half is None else half[None]
    rows = rows if half is None else rows // 2
    columns = right.shape[0] if transposed else right.shape[1]
    size = min(512, columns)
    if transposed:
        right_spec = pl.BlockSpec((size, depth), lambda j, at: (j, 0))
    else:
        right_spec = pl.BlockSpec((depth, size), lambda j, at: (0, j))
    specs = [pl.BlockSpec((rows, depth), lambda j, at: (at[0], 0)), right_spec]
    args = [left, right]
    if bias is not None:
        specs.append(pl.BlockSpec((1, size), lambda j, at: (0, j)))
        args.append(bias[None])
    return pl.pallas_call(
        functools.partial(matmul_kernel, NT if transposed else (((1,), (0,)), ((), ()))),
        grid_spec=pltpu.PrefetchScalarGridSpec(
            num_scalar_prefetch=1,
            grid=(columns // size,),
            in_specs=specs,
            out_specs=pl.BlockSpec((rows, size), lambda j, at: (0, j)),
        ),
        out_shape=jax.ShapeDtypeStruct((rows, columns), BF),
        compiler_params=pltpu.CompilerParams(vmem_limit_bytes=48 * 2**20),
        cost_estimate=BRIEF,
        name="brief_mm",
    )(at, *args)


def far_packed_kernel(count, order, *refs):
    out_ref = refs[-1]
    bias_ref = refs[-2]
    total = mm(refs[0][...], refs[count][...])
    for k in range(1, count):
        total = total + mm(refs[k][...], refs[count + k][...])
    out_ref[...] = (total + bias_ref[...]).astype(BF)


def brief_by_parts(rows, parts, bias):
    count = len(parts)
    depth, columns = parts[0].shape
    size = min(512, rows.shape[0])
    order = jnp.stack([lax.axis_index("dp") ^ k for k in range(count)])
    specs = [
        pl.BlockSpec((size, depth), functools.partial(lambda k, i, order: (i, order[k]), k))
        for k in range(count)
    ]
    specs += [pl.BlockSpec((depth, columns), lambda i, *_: (0, 0))] * count
    specs.append(pl.BlockSpec((1, columns), lambda i, *_: (0, 0)))
    return pl.pallas_call(
        functools.partial(far_packed_kernel, count),
        grid_spec=pltpu.PrefetchScalarGridSpec(
            num_scalar_prefetch=1,
            grid=(rows.shape[0] // size,),
            in_specs=specs,
            out_specs=pl.BlockSpec((size, columns), lambda i, *_: (i, 0)),
        ),
        out_shape=jax.ShapeDtypeStruct((rows.shape[0], columns), BF),
        compiler_params=pltpu.CompilerParams(vmem_limit_bytes=48 * 2**20),
        cost_estimate=BRIEF,
        name="brief_by_parts",
    )(order, *[rows] * count, *parts, bias[None])


def gelu_slope(hidden):
    square = hidden * hidden
    bend = jnp.tanh(0.7978845608 * hidden * (1.0 + 0.044715 * square))
    inner = 0.7978845608 * (1.0 + 3.0 * 0.044715 * square)
    return 0.5 * (1.0 + bend) + 0.5 * hidden * (1.0 - bend * bend) * inner


def unit_back_kernel(grad_ref, weight_ref, hidden_ref, out_ref):
    d_act = mm_nt(grad_ref[...], weight_ref[...])
    out_ref[...] = (d_act * gelu_slope(hidden_ref[...])).astype(BF)


def unit_back(grad, weight, hidden):
    rows, depth = grad.shape
    units = weight.shape[0]
    size = min(512, units)
    tile = pl.BlockSpec((rows, size), lambda j: (0, j))
    return pl.pallas_call(
        unit_back_kernel,
        grid=(units // size,),
        in_specs=[
            pl.BlockSpec((rows, depth), lambda j: (0, 0)),
            pl.BlockSpec((size, depth), lambda j: (j, 0)),
            tile,
        ],
        out_specs=tile,
        out_shape=jax.ShapeDtypeStruct((rows, units), BF),
        compiler_params=pltpu.CompilerParams(vmem_limit_bytes=48 * 2**20),
        cost_estimate=BRIEF,
        name="unit_back",
    )(grad, weight, hidden)


def grad_kernel(pairs, *refs):
    total = sum(mm_tn(refs[2 * i][...], refs[2 * i + 1][...]) for i in range(pairs))
    at = 0
    for out_ref in refs[2 * pairs :]:
        out_ref[...] = total[:, at : at + out_ref.shape[1]].astype(BF)
        at += out_ref.shape[1]


def brief_grad(pairs, widths):
    rows = pairs[0][0].shape[1]
    size = min(256, rows)
    specs = []
    args = []
    for left, right in pairs:
        specs.append(pl.BlockSpec((left.shape[0], size), lambda i: (0, i)))
        specs.append(pl.BlockSpec(right.shape, lambda i: (0, 0)))
        args += [left, right]
    return pl.pallas_call(
        functools.partial(grad_kernel, len(pairs)),
        grid=(rows // size,),
        in_specs=specs,
        out_specs=[pl.BlockSpec((size, width), lambda i: (i, 0)) for width in widths],
        out_shape=[jax.ShapeDtypeStruct((rows, width), BF) for width in widths],
        compiler_params=pltpu.CompilerParams(vmem_limit_bytes=52 * 2**20),
        cost_estimate=BRIEF,
        name="brief_grad",
    )(*args)


def norm_kernel(half, x_ref, gain_ref, shift_ref, out_ref):
    wide = x_ref[...].astype(F32)
    mean = jnp.mean(wide, axis=1, keepdims=True)
    centred = wide - mean
    inv = lax.rsqrt(jnp.mean(centred * centred, axis=1, keepdims=True) + EPSILON)
    out_ref[...] = (centred * inv * gain_ref[...] + shift_ref[...]).astype(BF)


def norm_rows(tokens, half, length, gain, shift):
    width = tokens.shape[1]
    size = 256
    steps = length // size
    vector = pl.BlockSpec((1, width), lambda i, *_: (0, 0))
    return pl.pallas_call(
        norm_kernel,
        grid_spec=pltpu.PrefetchScalarGridSpec(
            num_scalar_prefetch=1,
            grid=(steps,),
            in_specs=[
                pl.BlockSpec((size, width), lambda i, at: (at[0] * steps + i, 0)),
                vector,
                vector,
            ],
            out_specs=pl.BlockSpec((size, width), lambda i, at: (i, 0)),
        ),
        out_shape=jax.ShapeDtypeStruct((length, width), BF),
        compiler_params=pltpu.CompilerParams(vmem_limit_bytes=40 * 2**20),
        cost_estimate=BRIEF,
        name="norm_rows",
    )(half[None], tokens, gain[None], shift[None])


def gather_kernel(x_ref, pos_ref, out_ref):
    wanted = pos_ref[0]
    total = jnp.zeros(out_ref.shape, F32)
    for start in range(0, x_ref.shape[0], BK):
        here = start + lax.broadcasted_iota(jnp.int32, (BK, wanted.shape[1]), 0)
        total = total + mm_tn((here == wanted).astype(BF), x_ref[start : start + BK, :])
    out_ref[...] = total.astype(BF)


def gather_slots(values, positions, capacity, length):
    rows = positions.shape[0]
    width = values.shape[1]
    return pl.pallas_call(
        gather_kernel,
        grid=(rows,),
        in_specs=[
            pl.BlockSpec((length, width), lambda r: (r, 0)),
            pl.BlockSpec((1, 1, capacity), lambda r: (r, 0, 0)),
        ],
        out_specs=pl.BlockSpec((capacity, width), lambda r: (r, 0)),
        out_shape=jax.ShapeDtypeStruct((rows * capacity, width), BF),
        compiler_params=pltpu.CompilerParams(vmem_limit_bytes=40 * 2**20),
        cost_estimate=BRIEF,
        name="gather_slots",
    )(values, positions[:, None, :capacity])


def place_kernel(wide, at, slots_ref, slot_ref, base_ref, *refs):
    out_ref = refs[-1]
    capacity = slots_ref.shape[0]
    size, width = out_ref.shape
    here = lax.broadcasted_iota(jnp.int32, (capacity, size), 0)
    one = (here == slot_ref[0]).astype(BF)
    hit = mm_tn(one, jnp.ones((capacity, width), BF))
    result = jnp.where(hit > 0.5, mm_tn(one, slots_ref[...]), base_ref[...].astype(F32))
    if wide:
        result = result + refs[0][...].astype(F32)
    out_ref[...] = result.astype(out_ref.dtype)


def place_tokens(slot_values, slot, base, column, addend=None):
    rows, length = slot.shape
    width = slot_values.shape[1]
    capacity = slot_values.shape[0] // rows
    size = 512
    steps = length // size
    token_spec = pl.BlockSpec((size, width), lambda r, i, *_: (r * steps + i, 0))
    if base.shape[1] % 128 == 0 and width % 128 == 0:
        base_spec = pl.BlockSpec((size, width), lambda r, i, at: (r * steps + i, at[0]))
    else:
        base = lax.dynamic_slice_in_dim(base, column * width, width, 1)
        base_spec = token_spec
    out_type = BF if addend is None else F32
    extra = [] if addend is None else [addend]
    return pl.pallas_call(
        functools.partial(place_kernel, addend is not None),
        grid_spec=pltpu.PrefetchScalarGridSpec(
            num_scalar_prefetch=1,
            grid=(rows, steps),
            in_specs=[
                pl.BlockSpec((capacity, width), lambda r, i, *_: (r, 0)),
                pl.BlockSpec((1, 1, size), lambda r, i, *_: (r, 0, i)),
                base_spec,
            ]
            + [token_spec] * len(extra),
            out_specs=token_spec,
        ),
        out_shape=jax.ShapeDtypeStruct((rows * length, width), out_type),
        compiler_params=pltpu.CompilerParams(vmem_limit_bytes=40 * 2**20),
        cost_estimate=BRIEF,
        name="place_tokens",
    )(column[None], slot_values, slot[:, None, :], base, *extra)


def split_heads(pairs, heads):
    lane = lax.broadcasted_iota(jnp.int32, (pairs.shape[0], 128), 1)
    out = []
    for pair in range(heads // 2):
        part = pairs[:, 128 * pair : 128 * pair + 128]
        zero = jnp.zeros_like(part)
        out += [jnp.where(lane < 64, part, zero), jnp.where(lane < 64, zero, part)]
    return out


def merge_heads(parts, block):
    row = lax.broadcasted_iota(jnp.int32, (128, block), 0)
    return [
        jnp.where(row < 64, parts[2 * pair], parts[2 * pair + 1])
        for pair in range(len(parts) // 2)
    ]


def unpack(heads, packed_ref, q_all, k_all, v_all):
    lane = lax.broadcasted_iota(jnp.int32, (packed_ref.shape[0], 128), 1)
    for pair in range(heads // 2):
        lanes = slice(128 * pair, 128 * pair + 128)
        part = [packed_ref[:, 384 * pair + 128 * i : 384 * pair + 128 * i + 128] for i in range(3)]
        q_all[:, lanes] = jnp.where(lane < 64, part[0], part[1])
        keys = jnp.where(lane < 64, part[2], part[0])
        k_all[:, lanes] = pltpu.roll(keys.astype(F32), 64, 1).astype(BF)
        v_all[:, lanes] = jnp.where(lane < 64, part[1], part[2])


def attend_kernel(
    heads,
    first,
    last,
    near,
    packed_ref,
    lo_ref,
    hi_ref,
    o_ref,
    low_ref,
    lse_ref,
    q_ref,
    q_all,
    k_all,
    v_all,
):
    block = pl.program_id(0)

    @pl.when(block == 0)
    def _():
        unpack(heads, packed_ref, q_all, k_all, v_all)

    lo = lo_ref[...]
    hi = hi_ref[...]

    def pick_step(window, total):
        start = pl.multiple_of(window * BK, BK)
        here = start + lax.broadcasted_iota(jnp.int32, (BK, BQ), 0)
        return total + mm_tn((here == hi).astype(BF), q_all[pl.ds(start, BK), :])

    picked = lax.fori_loop(near[block], last[block], pick_step, jnp.zeros(q_ref.shape, F32))
    picked = picked.astype(BF)
    q_ref[...] = picked
    queries = split_heads(picked * jnp.asarray(SCALE, BF), heads)

    def step(key_block, carried):
        start = pl.multiple_of(key_block * BK, BK)
        key_pos = start + lax.broadcasted_iota(jnp.int32, (BK, BQ), 0)
        allowed = (key_pos >= lo) & (key_pos <= hi)
        raw = [
            mm_nt(k_all[pl.ds(start, BK), 128 * (h // 2) : 128 * (h // 2) + 128], queries[h])
            for h in range(heads)
        ]
        out = []
        for h in range(heads):
            values = v_all[pl.ds(start, BK), 128 * (h // 2) : 128 * (h // 2) + 128]
            top, total, mixed = carried[3 * h : 3 * h + 3]
            scores = jnp.where(allowed, raw[h], MASKED)
            new_top = jnp.maximum(top, jnp.max(scores, axis=0, keepdims=True))
            weights = jnp.exp(scores - new_top)
            fade = jnp.exp(top - new_top)
            total = total * fade + jnp.sum(weights, axis=0, keepdims=True)
            mixed = mixed * fade + mm_tn(values, weights.astype(BF))
            out += [new_top, total, mixed]
        return tuple(out)

    init = (
        jnp.full((1, BQ), MASKED, F32),
        jnp.zeros((1, BQ), F32),
        jnp.zeros((128, BQ), F32),
    ) * heads
    done = lax.fori_loop(first[block], last[block], step, init)
    merged = merge_heads([done[3 * h + 2] / done[3 * h + 1] for h in range(heads)], BQ)
    for pair in range(heads // 2):
        part = merged[pair].T
        o_ref[:, 128 * pair : 128 * pair + 128] = part
        low_ref[:, 128 * pair : 128 * pair + 128] = part.astype(BF)
    row = lax.broadcasted_iota(jnp.int32, (8, BQ), 0)
    lse = jnp.zeros((8, BQ), F32)
    for h in range(heads):
        lse = jnp.where(row == h, done[3 * h] + jnp.log(done[3 * h + 1]), lse)
    lse_ref[...] = lse


def attend(packed, lo, hi, bounds):
    count = hi.shape[1]
    length = packed.shape[0]
    width = packed.shape[1] // 3
    heads = width // HD
    row_spec = pl.BlockSpec((1, BQ), lambda i, *_: (0, i))
    block_spec = pl.BlockSpec((BQ, width), lambda i, *_: (i, 0))
    spec = pltpu.PrefetchScalarGridSpec(
        num_scalar_prefetch=3,
        grid=(count // BQ,),
        in_specs=[
            pl.BlockSpec((length, 3 * width), lambda i, *_: (0, 0)),
            row_spec,
            row_spec,
        ],
        out_specs=[
            block_spec,
            block_spec,
            pl.BlockSpec((8, BQ), lambda i, *_: (0, i)),
            block_spec,
        ],
        scratch_shapes=[pltpu.VMEM((length, width), BF)] * 3,
    )
    return pl.pallas_call(
        functools.partial(attend_kernel, heads),
        grid_spec=spec,
        out_shape=[
            jax.ShapeDtypeStruct((count, width), F32),
            jax.ShapeDtypeStruct((count, width), BF),
            jax.ShapeDtypeStruct((8, count), F32),
            jax.ShapeDtypeStruct((count, width), BF),
        ],
        compiler_params=pltpu.CompilerParams(vmem_limit_bytes=48 * 2**20),
        cost_estimate=BRIEF,
        name="attend",
    )(*bounds, packed, lo, hi)


def attend_back_kernel(
    heads,
    first,
    last,
    near,
    packed_ref,
    q_ref,
    g_ref,
    o_ref,
    lse_ref,
    lo_ref,
    hi_ref,
    *refs,
):
    out_ref, q_all, k_all, v_all, dq_sum, dk_sum, dv_sum = refs[-7:]
    count, width = q_ref.shape
    unpack(heads, packed_ref, q_all, k_all, v_all)
    dq_sum[...] = jnp.zeros_like(dq_sum)
    dk_sum[...] = jnp.zeros_like(dk_sum)
    dv_sum[...] = jnp.zeros_like(dv_sum)
    head_of = lax.broadcasted_iota(jnp.int32, (8, width), 1) // HD
    picks = (head_of == lax.broadcasted_iota(jnp.int32, (8, width), 0)).astype(F32)

    def query_step(block, _):
        at = pl.multiple_of(block * BQ, BQ)
        queries = split_heads(q_ref[pl.ds(at, BQ), :] * jnp.asarray(SCALE, BF), heads)
        grad = g_ref[pl.ds(at, BQ), :]
        grads = split_heads(grad, heads)
        lo = lo_ref[:, pl.ds(at, BQ)]
        hi = hi_ref[:, pl.ds(at, BQ)]
        delta = lax.dot_general(
            picks,
            grad.astype(F32) * o_ref[pl.ds(at, BQ), :],
            NT,
            precision=lax.Precision.HIGHEST,
            preferred_element_type=F32,
        )

        def key_step(key_block, carried):
            start = pl.multiple_of(key_block * BK, BK)
            key_pos = start + lax.broadcasted_iota(jnp.int32, (BK, BQ), 0)
            allowed = (key_pos >= lo) & (key_pos <= hi)
            out = []
            for pair in range(heads // 2):
                lanes = slice(128 * pair, 128 * pair + 128)
                keys = k_all[pl.ds(start, BK), lanes]
                values = v_all[pl.ds(start, BK), lanes]
                dk = dk_sum[pl.ds(start, BK), lanes]
                dv = dv_sum[pl.ds(start, BK), lanes]
                for h in (2 * pair, 2 * pair + 1):
                    scores = mm_nt(keys, queries[h])
                    shares = jnp.exp(
                        jnp.where(allowed, scores, MASKED) - lse_ref[h : h + 1, pl.ds(at, BQ)]
                    )
                    d_shares = mm_nt(values, grads[h])
                    d_scores = (shares * (d_shares - delta[h : h + 1, :])).astype(BF)
                    dv = dv + mm(shares.astype(BF), grads[h])
                    dk = dk + mm(d_scores, queries[h])
                    out.append(carried[h] + mm_tn(keys, d_scores))
                dk_sum[pl.ds(start, BK), lanes] = dk
                dv_sum[pl.ds(start, BK), lanes] = dv
            return tuple(out)

        done = lax.fori_loop(
            first[block], last[block], key_step, (jnp.zeros((128, BQ), F32),) * heads
        )
        d_queries = [(part.T * SCALE).astype(BF) for part in merge_heads(done, BQ)]

        def place_step(window, _):
            start = pl.multiple_of(window * BK, BK)
            here = start + lax.broadcasted_iota(jnp.int32, (BK, BQ), 0)
            one = (here == hi).astype(BF)
            for pair in range(heads // 2):
                lanes = slice(128 * pair, 128 * pair + 128)
                dq_sum[pl.ds(start, BK), lanes] += mm(one, d_queries[pair])
            return 0

        lax.fori_loop(near[block], last[block], place_step, 0)
        return 0

    lax.fori_loop(0, count // BQ, query_step, 0)
    lane = lax.broadcasted_iota(jnp.int32, (out_ref.shape[0], 128), 1)
    for pair in range(heads // 2):
        lanes = slice(128 * pair, 128 * pair + 128)
        dq = dq_sum[:, lanes]
        dk = pltpu.roll(dk_sum[:, lanes], 64, 1)
        dv = dv_sum[:, lanes]
        merged = (
            jnp.where(lane < 64, dq, dk),
            jnp.where(lane < 64, dv, dq),
            jnp.where(lane < 64, dk, dv),
        )
        for i, part in enumerate(merged):
            out_ref[:, 384 * pair + 128 * i : 384 * pair + 128 * i + 128] = part.astype(BF)


def attend_back(packed, queries, grads, column, mixed, lse, lo, hi, bounds, sets, joined):
    count, width = queries.shape
    length = packed.shape[0]
    heads = width // HD
    query_spec = pl.BlockSpec((count, width), lambda i, *_: (0, 0))
    grad_spec = pl.BlockSpec((count, width), lambda i, *_: (0, column))
    packed_spec = pl.BlockSpec((length, 3 * width), lambda i, *_: (0, 0))
    row_spec = pl.BlockSpec((1, count), lambda i, *_: (0, 0))
    spec = pltpu.PrefetchScalarGridSpec(
        num_scalar_prefetch=3,
        grid=(1,),
        in_specs=[
            packed_spec,
            query_spec,
            grad_spec,
            query_spec,
            pl.BlockSpec((8, count), lambda i, *_: (0, 0)),
            row_spec,
            row_spec,
        ]
        + [pl.BlockSpec(memory_space=pl.ANY)] * (joined is not None),
        out_specs=pl.BlockSpec((length, 3 * width), lambda i, *_: (0, column)),
        scratch_shapes=[pltpu.VMEM((length, width), BF)] * 3
        + [pltpu.VMEM((length, width), F32)] * 3,
    )
    return pl.pallas_call(
        functools.partial(attend_back_kernel, heads),
        grid_spec=spec,
        out_shape=jax.ShapeDtypeStruct((length, 3 * width * sets), BF),
        input_output_aliases={} if joined is None else {10: 0},
        compiler_params=pltpu.CompilerParams(vmem_limit_bytes=58 * 2**20),
        cost_estimate=BRIEF,
        name="attend_back",
    )(*bounds, packed, queries, grads, mixed, lse, lo, hi, *([] if joined is None else [joined]))


def swap_halves(value):
    return lax.ppermute(value, "half", [(0, 1), (1, 0)])


def swap_by_gather(value):
    rows = value.shape[0]
    pair = lax.all_gather(value, "half", axis=0, tiled=True)
    return lax.dynamic_slice_in_dim(pair, (1 - lax.axis_index("half")) * rows, rows, 0)


def exchange(value, bit, axis="tp"):
    return lax.ppermute(value, axis, [(i, i ^ bit) for i in range(lax.axis_size(axis))])


def gather_near(value):
    bit = 1
    while bit < lax.axis_size("tp") // 2:
        value = jnp.concatenate((value, exchange(value, bit)), axis=0)
        bit *= 2
    return value


def send_top(value):
    return exchange(value, lax.axis_size("tp") // 2)


def fold_tp(value, *beside):
    bit = lax.axis_size("tp") // 4
    while bit:
        rows = value.shape[0] // 2
        received = tie(exchange(value[rows:].astype(BF), bit), *beside)
        value = value[:rows].astype(F32) + received.astype(F32)
        bit //= 2
    return value.astype(F32)


def fold_natural(value):
    bit = lax.axis_size("tp") // 4
    place = lax.axis_index("tp")
    while bit:
        rows = value.shape[0] // 2
        mine = (place // bit) % 2
        kept = lax.dynamic_slice_in_dim(value, mine * rows, rows, 0)
        sent = lax.dynamic_slice_in_dim(value, (1 - mine) * rows, rows, 0)
        value = kept.astype(F32) + exchange(sent.astype(BF), bit).astype(F32)
        bit //= 2
    return value.astype(F32)


def natural_halves(value):
    rows = value.shape[0] // 2
    top = lax.axis_index("tp") // (lax.axis_size("tp") // 2)
    return (
        lax.dynamic_slice_in_dim(value, top * rows, rows, 0),
        lax.dynamic_slice_in_dim(value, (1 - top) * rows, rows, 0),
    )


def relative_rows(value):
    count = lax.axis_size("tp")
    size = value.shape[0] // count
    place = lax.axis_index("tp")
    blocks = [
        lax.dynamic_slice_in_dim(value, (place ^ k) * size, size, 0) for k in range(count)
    ]
    middle = count // 2
    return jnp.concatenate(blocks[:middle], axis=0), jnp.concatenate(blocks[middle:], axis=0)


def both(parts):
    return jnp.concatenate(parts, axis=0)


def own_dp_part(weight):
    part = weight.shape[0] // lax.axis_size("dp")
    return lax.dynamic_slice_in_dim(weight, lax.axis_index("dp") * part, part, 0)


def spread_first(part):
    return exchange(part, 1, "dp"), exchange(part, 2, "dp")


def spread_second(part, first):
    count = lax.axis_size("dp")
    one, two = first
    middle = part.shape[0] // 2
    blocks = [(0, 0, part), (1, 0, one), (2, 0, two)]
    blocks.append((3, 0, exchange(two[:middle], 1, "dp")))
    blocks.append((3, middle, exchange(one[middle:], 2, "dp")))
    bit = 4
    while bit < count:
        blocks = blocks + [(k + bit, at, exchange(block, bit, "dp")) for k, at, block in blocks]
        bit *= 2
    return blocks


def whole_parts(blocks):
    parts = {}
    for k, _, block in blocks:
        parts.setdefault(k, []).append(block)
    return [jnp.concatenate(parts[k], axis=0) for k in range(len(parts))]


def assemble(buffer, blocks, row, column):
    member = lax.axis_index("dp")
    size = buffer.shape[0] - row
    part = size // lax.axis_size("dp")
    for k, offset, block in blocks:
        start = row + (member ^ k) * part + offset
        buffer = lax.dynamic_update_slice(buffer, block, (start, column))
    return buffer


def sum_over_dp(grad, dimension):
    return lax.psum_scatter(grad.astype(BF), "dp", scatter_dimension=dimension, tiled=True)


ALL = ("half", "tp")


def running_count(flags):
    rows, length = flags.shape
    chunk = 128
    tiles = flags.reshape(rows, length // chunk, chunk)
    ones = (
        lax.broadcasted_iota(jnp.int32, (chunk, chunk), 0)
        <= lax.broadcasted_iota(jnp.int32, (chunk, chunk), 1)
    ).astype(BF)
    inside = jnp.einsum("rtc,cd->rtd", tiles.astype(BF), ones, preferred_element_type=F32)
    totals = jnp.sum(tiles, axis=2)
    tile_count = length // chunk
    earlier = (
        lax.broadcasted_iota(jnp.int32, (tile_count, tile_count), 0)
        < lax.broadcasted_iota(jnp.int32, (tile_count, tile_count), 1)
    ).astype(F32)
    before = jnp.sum(totals[:, :, None] * earlier[None], axis=1)
    return (inside + before[:, :, None]).reshape(rows, length)


def prepare(
    tokens,
    segment_ids,
    exit_layer,
    norm1_gain,
    norm1_shift,
    w_qkv,
    b_qv,
    w_out,
    b_out,
    norm2_gain,
    norm2_shift,
    w_up,
    b_up,
    w_down,
    b_down,
    cotangent,
):
    half = lax.axis_index("half")
    rows, length = segment_ids.shape
    own_heads = b_qv.shape[0] // (2 * HD)

    far_qkv_part = swap_halves(own_dp_part(w_qkv))
    far_vectors = swap_halves(jnp.concatenate((b_qv, b_up, b_out, b_down)))

    active = exit_layer > LAYER
    most = jnp.max(jnp.sum(active.astype(F32), axis=1)) * jnp.ones((8, 128), F32)
    bit = 1
    while bit < lax.axis_size("dp"):
        most = jnp.maximum(most, exchange(most, bit, "dp"))
        bit *= 2

    normed1 = norm_rows(
        tokens, half, length, norm1_gain.astype(F32), norm1_shift.astype(F32)
    )
    own_packed = (mm(normed1, w_qkv) + qkv_bias(b_qv)).astype(BF)

    running = running_count(active.astype(F32)).astype(jnp.int32)
    slot = jnp.where(active, running - 1, -1)
    slots = lax.broadcasted_iota(jnp.int32, (1, length, 1), 1)
    positions = jnp.sum((running[:, None, :] <= slots).astype(jnp.int32), axis=2)
    own_positions = lax.dynamic_index_in_dim(positions, half, 0, keepdims=False)
    own_docs = lax.dynamic_index_in_dim(segment_ids, half, 0, keepdims=False)
    doc_numbers = jnp.arange(DOCS, dtype=jnp.int32)[:, None]
    doc_starts = jnp.sum((own_docs[None, :] < doc_numbers).astype(jnp.int32), axis=1, keepdims=True)
    hi = jnp.minimum(own_positions, length - 1)
    lo = jnp.max(jnp.where(doc_starts <= hi[None, :], doc_starts, 0), axis=0)
    prepared = (far_qkv_part, far_vectors, normed1, own_packed, slot, positions, own_positions, lo, hi)
    return most[0, 0], prepared


def qkv_bias(bias):
    pairs = bias.astype(F32).reshape(-1, 2, HD)
    zero = jnp.zeros_like(pairs[:, 0])
    return jnp.stack((pairs[:, 0], zero, pairs[:, 1]), axis=1).reshape(-1)


def layer(
    capacity,
    prepared,
    tokens,
    segment_ids,
    exit_layer,
    norm1_gain,
    norm1_shift,
    w_qkv,
    b_qv,
    w_out,
    b_out,
    norm2_gain,
    norm2_shift,
    w_up,
    b_up,
    w_down,
    b_down,
    cotangent,
):
    far_qkv_part, far_vectors, normed1, own_packed, slot, positions, own_positions, lo, hi = prepared
    n_tp = lax.axis_size("tp")
    half = lax.axis_index("half")
    place = lax.axis_index("tp")
    rows, length = segment_ids.shape
    width = tokens.shape[1]
    own_width = cotangent.shape[1]
    device = half * n_tp + place
    own_heads = b_qv.shape[0] // (2 * HD)
    units = w_up.shape[1]
    cap_all = -(-capacity // BQ) * BQ
    cap_part = capacity // n_tp
    part = length // n_tp
    gain1 = norm1_gain.astype(F32)

    lo = lo[:cap_all]
    hi = hi[:cap_all]
    bounds = (lo[::BQ] // BK, hi[BQ - 1 :: BQ] // BK + 1, hi[::BQ] // BK)
    lo = lo[None]
    hi = hi[None]

    size = b_qv.shape[0]
    far_b_qv = far_vectors[:size]
    far_b_up = far_vectors[size : size + units]
    far_b_out = far_vectors[size + units : size + units + own_width]
    far_b_down = far_vectors[size + units + own_width :]

    def share_of_bias(own, far):
        bias = jnp.zeros((width,), F32)
        bias = lax.dynamic_update_slice(bias, own.astype(F32), (device * own_width,))
        other = (1 - half) * n_tp + place
        return lax.dynamic_update_slice(bias, far.astype(F32), (other * own_width,))

    far_qkv_first = spread_first(far_qkv_part)
    far_out_part = swap_halves(own_dp_part(w_out))
    own_cot = gather_slots(cotangent, positions, capacity, length)
    cot = lax.all_to_all(own_cot, ALL, split_axis=0, concat_axis=1, tiled=True)

    if own_heads % 2:
        far_qkv_blocks = spread_second(far_qkv_part, far_qkv_first)
        far_qkv = assemble(jnp.zeros_like(w_qkv), far_qkv_blocks, 0, 0)
        far_packed = (mm(normed1, far_qkv) + qkv_bias(far_b_qv)).astype(BF)
        packs = [jnp.concatenate((own_packed, far_packed), axis=1)]
        far_cot = send_top(cot)
        far_up_part = swap_halves(own_dp_part(w_up))
        kept = [attend(packs[0], lo, hi, bounds)]
    else:
        own_kept = attend(own_packed, lo, hi, bounds)
        far_qkv_first, *own_kept = lax.optimization_barrier((far_qkv_first, *own_kept))
        far_qkv_blocks = spread_second(far_qkv_part, far_qkv_first)
        far_up_part = swap_by_gather(own_dp_part(w_up))
        far_packed = brief_by_parts(normed1, whole_parts(far_qkv_blocks), qkv_bias(far_b_qv))
        cot, far_out_part, far_packed = lax.optimization_barrier((cot, far_out_part, far_packed))
        far_cot = send_top(cot)
        packs = [own_packed, far_packed]
        kept = [own_kept, attend(far_packed, lo, hi, bounds)]
    far_out = lax.all_gather(far_out_part, "dp", axis=0, tiled=True)
    far_up_part, far_cot, head_out = lax.optimization_barrier(
        (far_up_part, far_cot, jnp.concatenate([item[1] for item in kept], axis=1))
    )
    far_up_first = spread_first(far_up_part)
    far_down_part = swap_by_gather(tie(own_dp_part(w_down), far_up_part))

    out_weight = jnp.concatenate((w_out, far_out), axis=0)
    head_out = head_out[:capacity]
    near_rows, far_rows = natural_halves(head_out)
    out_bias = share_of_bias(b_out, far_b_out)
    far_branch = fold_natural((mm(far_rows, out_weight) + out_bias).astype(BF)).astype(BF)
    near_branch = fold_natural((mm(near_rows, out_weight) + out_bias).astype(BF))
    recv_branch = send_top(far_branch)
    part_positions = lax.dynamic_slice_in_dim(own_positions, place * cap_part, cap_part)
    part_pick = (
        part_positions[:, None] == lax.broadcasted_iota(jnp.int32, (1, length), 1)
    ).astype(BF)
    own_inputs = lax.dynamic_slice_in_dim(tokens, half * length, length, 0)
    part_inputs = mm(tie(part_pick, far_branch), own_inputs).astype(BF)
    qkv_weight = assemble(
        jnp.pad(tie(w_qkv, far_branch), ((0, 0), (0, w_qkv.shape[1]))),
        far_qkv_blocks,
        0,
        w_qkv.shape[1],
    )
    up_weight = jnp.pad(tie(w_up, far_branch), ((0, 0), (0, units)))
    near_d_ffn = gather_near(cot)
    far_d_ffn = gather_near(far_cot)
    recv_branch, near_branch, part_inputs, far_up_first, up_weight, qkv_weight = (
        lax.optimization_barrier(
            (recv_branch, near_branch, part_inputs, far_up_first, up_weight, qkv_weight)
        )
    )
    far_up_blocks = spread_second(far_up_part, far_up_first)
    residual = part_inputs.astype(F32) + near_branch + recv_branch.astype(F32)
    mean2 = jnp.mean(residual, axis=1, keepdims=True)
    inv2 = lax.rsqrt(jnp.mean(jnp.square(residual - mean2), axis=1, keepdims=True) + EPSILON)
    standard2 = (residual - mean2) * inv2
    gain2 = norm2_gain.astype(F32)
    part_normed2 = (standard2 * gain2 + norm2_shift.astype(F32)).astype(BF)
    near_normed2 = gather_near(part_normed2)
    far_normed2 = send_top(part_normed2)
    up_weight = assemble(up_weight, far_up_blocks, 0, units)
    down_weight = jnp.pad(tie(w_down, part_normed2), ((0, units), (0, 0)))
    up_bias = jnp.concatenate((b_up, far_b_up)).astype(F32)

    def forward(part_in):
        hidden = mm(part_in, up_weight) + up_bias
        return jax.nn.gelu(hidden, approximate=True).astype(BF), hidden

    near_act, near_hidden = forward(near_normed2)
    far_down_part, near_act = lax.optimization_barrier((far_down_part, near_act))
    far_down_first = spread_first(far_down_part)
    far_normed2, near_act = lax.optimization_barrier((far_normed2, near_act))
    far_normed2 = gather_near(far_normed2)
    far_act, far_hidden = forward(far_normed2)
    down_weight = assemble(
        down_weight, spread_second(far_down_part, far_down_first), units, 0
    )
    down_weight, far_act = lax.optimization_barrier((down_weight, far_act))
    far_d_hidden = (mm_nt(far_d_ffn, down_weight) * gelu_slope(far_hidden)).astype(BF)
    down_bias = share_of_bias(b_down, far_b_down)
    far_d_normed2 = mm_nt(far_d_hidden, up_weight).astype(BF)
    far_ffn = (mm(tie(far_act, far_d_normed2), down_weight) + down_bias).astype(BF)
    far_d_normed2 = fold_tp(far_d_normed2, far_ffn).astype(BF)
    recv_d_normed2 = send_top(far_d_normed2)
    (grad_down,) = brief_grad(
        ((tie(near_act, far_d_normed2), near_d_ffn), (far_act, far_d_ffn)), (width,)
    )
    near_d_hidden = unit_back(tie(near_d_ffn, grad_down), down_weight, near_hidden)
    near_d_normed2 = brief_mm(near_d_hidden, up_weight, None, True)
    recv_d_normed2, near_d_normed2, grad_down = lax.optimization_barrier(
        (recv_d_normed2, near_d_normed2, grad_down)
    )
    near_d_normed2 = fold_tp(near_d_normed2)
    grad_down = sum_over_dp(grad_down.reshape(2, units, width), 2)

    d_normed2 = near_d_normed2 + recv_d_normed2.astype(F32)
    g2 = d_normed2 * gain2
    d_residual = cot.astype(F32) + inv2 * (
        g2
        - jnp.mean(g2, axis=1, keepdims=True)
        - standard2 * jnp.mean(g2 * standard2, axis=1, keepdims=True)
    )
    d_branch_part = d_residual.astype(BF)
    far_d_branch = send_top(d_branch_part)
    near_d_branch = gather_near(d_branch_part)
    near_d_heads = brief_mm(near_d_branch, out_weight, None, True)
    near_ffn = brief_mm(tie(near_act, near_d_heads), down_weight, down_bias)
    (grad_up,) = brief_grad(
        ((tie(near_normed2, near_ffn), near_d_hidden), (far_normed2, far_d_hidden)), (2 * units,)
    )
    far_d_branch, grad_up, near_ffn = lax.optimization_barrier((far_d_branch, grad_up, near_ffn))
    far_ffn = fold_tp(tie(far_ffn, far_d_branch)).astype(BF)
    near_ffn = fold_tp(tie(near_ffn, far_d_branch))
    recv_ffn = send_top(far_ffn)
    far_d_branch = gather_near(far_d_branch)
    d_heads = both((near_d_heads, mm_nt(far_d_branch, out_weight).astype(BF)))
    d_heads = jnp.pad(both(relative_rows(d_heads)), ((0, cap_all - capacity), (0, 0)))
    d_heads, grad_down = lax.optimization_barrier((d_heads, grad_down))
    grad_up = sum_over_dp(tie(grad_up, grad_down), 0)
    far_swap_down = swap_halves(grad_down[1])
    def back(at, joined):
        item = kept[at]
        return attend_back(
            packs[at], item[3], d_heads, at, item[0], item[2], lo, hi, bounds, len(packs), joined
        )

    d_pack = back(0, None)
    head_rows = relative_rows(head_out)
    (grad_out,) = brief_grad(
        ((tie(head_rows[0], d_pack), near_d_branch), (head_rows[1], far_d_branch)), (width,)
    )
    d_pack, grad_out, recv_ffn, far_swap_down = lax.optimization_barrier(
        (d_pack, grad_out, recv_ffn, far_swap_down)
    )
    out_part = (residual + near_ffn + recv_ffn.astype(F32)).astype(BF)
    slot_parts = jnp.concatenate((d_branch_part, out_part), axis=0)
    slot_parts = lax.all_to_all(slot_parts, ALL, split_axis=1, concat_axis=0, tiled=True)
    if len(packs) == 2:
        d_pack = back(1, tie(d_pack, out_part))
    d_pack, grad_up = lax.optimization_barrier((d_pack, grad_up))
    far_swap_up = swap_halves(grad_up[:, units:])
    grad_out = sum_over_dp(tie(grad_out, grad_up), 1)
    top = place // (n_tp // 2)
    far_d_normed1 = brief_mm(d_pack, qkv_weight, None, True, 1 - top)
    far_d_normed1 = fold_natural(far_d_normed1).astype(BF)
    recv_d_normed1 = send_top(far_d_normed1)
    near_d_normed1 = brief_mm(tie(d_pack, far_d_normed1), qkv_weight, None, True, top)
    qkv_width = w_qkv.shape[1]
    own_grad_qkv, far_grad_qkv = brief_grad(
        ((tie(normed1, near_d_normed1), d_pack),), (qkv_width, qkv_width)
    )
    recv_d_normed1, near_d_normed1, own_grad_qkv, far_grad_qkv, grad_out, slot_parts = (
        lax.optimization_barrier(
            (recv_d_normed1, near_d_normed1, own_grad_qkv, far_grad_qkv, grad_out, slot_parts)
        )
    )
    slot_parts = slot_parts.reshape(-1, 2, cap_part, own_width)
    d_residual_slots = slot_parts[:, 0].reshape(-1, own_width)
    out_slots = slot_parts[:, 1].reshape(-1, own_width)
    near_d_normed1 = fold_natural(near_d_normed1)
    far_grad_qkv = sum_over_dp(far_grad_qkv, 0)

    part_tokens = lax.dynamic_slice_in_dim(tokens, half * length + place * part, part, 0)
    part_tokens = part_tokens.astype(F32)
    mean1 = jnp.mean(part_tokens, axis=1, keepdims=True)
    centred1 = part_tokens - mean1
    inv1 = lax.rsqrt(jnp.mean(centred1 * centred1, axis=1, keepdims=True) + EPSILON)
    standard1 = centred1 * inv1
    d_normed1 = near_d_normed1 + recv_d_normed1.astype(F32)
    g1 = d_normed1 * gain1
    d_norm1 = inv1 * (
        g1
        - jnp.mean(g1, axis=1, keepdims=True)
        - standard1 * jnp.mean(g1 * standard1, axis=1, keepdims=True)
    )
    d_norm1_part = d_norm1.astype(BF)
    d_norm1_tokens = lax.all_to_all(
        d_norm1_part, ALL, split_axis=1, concat_axis=0, tiled=True
    )
    result = place_tokens(out_slots, tie(slot, d_norm1_part), tokens, device)
    far_grad_qkv, far_swap_up, result = lax.optimization_barrier(
        (far_grad_qkv, far_swap_up, result)
    )
    own_grad_qkv = sum_over_dp(tie(own_grad_qkv, far_grad_qkv), 0)
    far_swap_qkv = swap_halves(far_grad_qkv)
    d_inputs = place_tokens(
        d_residual_slots, slot, cotangent, jnp.zeros_like(device), d_norm1_tokens
    )

    def join(own, far):
        return own.astype(F32) + far.astype(F32)

    grad_down = join(grad_down[0], far_swap_down)
    grad_up = join(grad_up[:, :units], far_swap_up)
    out_rows = w_out.shape[0]
    grad_out = join(grad_out[:out_rows], swap_halves(grad_out[out_rows:]))
    grad_qkv = join(own_grad_qkv, far_swap_qkv)

    d_hidden_sums = sum(
        jnp.sum(tie(item, d_norm1_part).astype(F32), axis=0)
        for item in (near_d_hidden, far_d_hidden)
    )
    d_pack_sums = jnp.sum(d_pack.astype(F32), axis=0).reshape(2, own_heads, 3, HD)
    d_bias_sums = jnp.stack((d_pack_sums[:, :, 0], d_pack_sums[:, :, 2]), axis=2).reshape(2, -1)
    unit_sums = jnp.concatenate((d_bias_sums[0], d_hidden_sums[:units])) + swap_halves(
        jnp.concatenate((d_bias_sums[1], d_hidden_sums[units:]))
    )
    late_d_normed1 = tie(d_normed1, d_norm1_part)
    late_d_normed2 = tie(d_normed2, d_norm1_part)
    features = jnp.stack(
        (
            jnp.sum(late_d_normed1 * standard1, axis=0),
            jnp.sum(late_d_normed1, axis=0),
            jnp.sum(late_d_normed2 * standard2, axis=0),
            jnp.sum(late_d_normed2, axis=0),
            jnp.sum(tie(d_branch_part, d_norm1_part).astype(F32), axis=0),
            jnp.sum(tie(cot, d_norm1_part).astype(F32), axis=0),
        )
    )
    features = tie(features, d_norm1_tokens)
    spread = lax.all_to_all(features, ALL, split_axis=1, concat_axis=0, tiled=True)
    feature_sums = jnp.sum(spread.reshape(-1, 6, own_width), axis=0).reshape(-1)
    summed = lax.psum(jnp.concatenate((feature_sums, unit_sums)), "dp")
    feature_sums = summed[: 6 * own_width].reshape(6, own_width)
    unit_sums = summed[6 * own_width :]
    return (
        result,
        d_inputs,
        feature_sums[0],
        feature_sums[1],
        grad_qkv,
        unit_sums[:size],
        grad_out,
        feature_sums[4],
        feature_sums[2],
        feature_sums[3],
        grad_up,
        unit_sums[size:],
        grad_down,
        feature_sums[5],
    )


def per_device(*args):
    length = args[2].shape[1]
    small = length * 11 // 16
    most, prepared = prepare(*args)
    return lax.cond(
        most <= small,
        functools.partial(layer, small),
        functools.partial(layer, length),
        prepared,
        *args,
    )


def solution(mesh):
    split = Mesh(mesh.devices.reshape(mesh.shape["dp"], 2, -1), ("dp", "half", "tp"))
    tensor = ("half", "tp")
    return jax.shard_map(
        per_device,
        mesh=split,
        in_specs=(
            P("dp", None),
            P("dp", None),
            P("dp", None),
            P(),
            P(),
            P(None, tensor),
            P(tensor),
            P(tensor, None),
            P(tensor),
            P(),
            P(),
            P(None, tensor),
            P(tensor),
            P(tensor, None),
            P(tensor),
            P("dp", tensor),
        ),
        out_specs=(
            P("dp", tensor),
            P("dp", tensor),
            P(tensor),
            P(tensor),
            P("dp", tensor),
            P(tensor),
            P(tensor, "dp"),
            P(tensor),
            P(tensor),
            P(tensor),
            P("dp", tensor),
            P(tensor),
            P(tensor, "dp"),
            P(tensor),
        ),
        check_vma=False,
    )
```

```python
import functools

import jax
import jax.numpy as jnp
from jax import lax
from jax.experimental import pallas as pl
from jax.experimental.pallas import tpu as pltpu
from jax.sharding import Mesh, PartitionSpec as P

HD = 64
LAYER = 8
DOCS = 6
EPSILON = 1e-05
MASKED = -1e30
SCALE = HD ** (-0.5)
F32 = jnp.float32
BF = jnp.bfloat16

BQ = 256
BK = 512

BRIEF = pl.CostEstimate(flops=1, bytes_accessed=1, transcendentals=0)

NT = (((1,), (1,)), ((), ()))
TN = (((0,), (0,)), ((), ()))


def mm(left, right):
    return jnp.dot(left, right, preferred_element_type=F32)


def mm_nt(left, right):
    return lax.dot_general(left, right, NT, preferred_element_type=F32)


def mm_tn(left, right):
    return lax.dot_general(left, right, TN, preferred_element_type=F32)


def tie(value, *others):
    return lax.optimization_barrier((value, *others))[0]


def matmul_kernel(dims, at, left_ref, right_ref, *refs):
    out = lax.dot_general(left_ref[...], right_ref[...], dims, preferred_element_type=F32)
    if len(refs) == 2:
        out = out + refs[0][...]
    refs[-1][...] = out.astype(BF)


def brief_mm(left, right, bias=None, transposed=False, half=None):
    rows, depth = left.shape
    at = jnp.zeros((1,), jnp.int32) if half is None else half[None]
    rows = rows if half is None else rows // 2
    columns = right.shape[0] if transposed else right.shape[1]
    size = min(512, columns)
    if transposed:
        right_spec = pl.BlockSpec((size, depth), lambda j, at: (j, 0))
    else:
        right_spec = pl.BlockSpec((depth, size), lambda j, at: (0, j))
    specs = [pl.BlockSpec((rows, depth), lambda j, at: (at[0], 0)), right_spec]
    args = [left, right]
    if bias is not None:
        specs.append(pl.BlockSpec((1, size), lambda j, at: (0, j)))
        args.append(bias[None])
    return pl.pallas_call(
        functools.partial(matmul_kernel, NT if transposed else (((1,), (0,)), ((), ()))),
        grid_spec=pltpu.PrefetchScalarGridSpec(
            num_scalar_prefetch=1,
            grid=(columns // size,),
            in_specs=specs,
            out_specs=pl.BlockSpec((rows, size), lambda j, at: (0, j)),
        ),
        out_shape=jax.ShapeDtypeStruct((rows, columns), BF),
        compiler_params=pltpu.CompilerParams(vmem_limit_bytes=48 * 2**20),
        cost_estimate=BRIEF,
        name="brief_mm",
    )(at, *args)


def pair_mm_kernel(at, one_ref, two_ref, right_ref, bias_ref, kept_ref, sent_ref):
    kept_ref[...] = (mm_nt(one_ref[...], right_ref[...]) + bias_ref[...]).astype(BF)
    sent_ref[...] = (mm_nt(two_ref[...], right_ref[...]) + bias_ref[...]).astype(BF)


def pair_mm(left, right, kept, sent):
    rows, depth = left.shape
    rows = rows // 4
    columns = right.shape[0]
    size = min(512, columns)
    out = pl.BlockSpec((rows, size), lambda j, at: (0, j))
    return pl.pallas_call(
        pair_mm_kernel,
        grid_spec=pltpu.PrefetchScalarGridSpec(
            num_scalar_prefetch=1,
            grid=(columns // size,),
            in_specs=[
                pl.BlockSpec((rows, depth), lambda j, at: (at[0], 0)),
                pl.BlockSpec((rows, depth), lambda j, at: (at[1], 0)),
                pl.BlockSpec((size, depth), lambda j, at: (j, 0)),
                pl.BlockSpec((1, size), lambda j, at: (0, j)),
            ],
            out_specs=[out, out],
        ),
        out_shape=[jax.ShapeDtypeStruct((rows, columns), BF)] * 2,
        compiler_params=pltpu.CompilerParams(vmem_limit_bytes=48 * 2**20),
        cost_estimate=BRIEF,
        name="pair_mm",
    )(jnp.stack((kept, sent)), left, left, right, jnp.zeros((1, columns), F32))


def add_kernel(one_ref, two_ref, out_ref):
    out_ref[...] = (one_ref[...].astype(F32) + two_ref[...].astype(F32)).astype(BF)


def brief_add(one, two):
    rows, width = one.shape
    size = min(512, width)
    tile = pl.BlockSpec((rows, size), lambda j: (0, j))
    return pl.pallas_call(
        add_kernel,
        grid=(width // size,),
        in_specs=[tile, tile],
        out_specs=tile,
        out_shape=jax.ShapeDtypeStruct(one.shape, BF),
        compiler_params=pltpu.CompilerParams(vmem_limit_bytes=40 * 2**20),
        cost_estimate=BRIEF,
        name="brief_add",
    )(one, two)


def far_packed_kernel(count, order, *refs):
    out_ref = refs[-1]
    bias_ref = refs[-2]
    total = mm(refs[0][...], refs[count][...])
    for k in range(1, count):
        total = total + mm(refs[k][...], refs[count + k][...])
    out_ref[...] = (total + bias_ref[...]).astype(BF)


def brief_by_parts(rows, parts, bias):
    count = len(parts)
    depth, columns = parts[0].shape
    size = min(512, rows.shape[0])
    order = jnp.stack([lax.axis_index("dp") ^ k for k in range(count)])
    specs = [
        pl.BlockSpec((size, depth), functools.partial(lambda k, i, order: (i, order[k]), k))
        for k in range(count)
    ]
    specs += [pl.BlockSpec((depth, columns), lambda i, *_: (0, 0))] * count
    specs.append(pl.BlockSpec((1, columns), lambda i, *_: (0, 0)))
    return pl.pallas_call(
        functools.partial(far_packed_kernel, count),
        grid_spec=pltpu.PrefetchScalarGridSpec(
            num_scalar_prefetch=1,
            grid=(rows.shape[0] // size,),
            in_specs=specs,
            out_specs=pl.BlockSpec((size, columns), lambda i, *_: (i, 0)),
        ),
        out_shape=jax.ShapeDtypeStruct((rows.shape[0], columns), BF),
        compiler_params=pltpu.CompilerParams(vmem_limit_bytes=48 * 2**20),
        cost_estimate=BRIEF,
        name="brief_by_parts",
    )(order, *[rows] * count, *parts, bias[None])


def gelu_slope(hidden):
    square = hidden * hidden
    bend = jnp.tanh(0.7978845608 * hidden * (1.0 + 0.044715 * square))
    inner = 0.7978845608 * (1.0 + 3.0 * 0.044715 * square)
    return 0.5 * (1.0 + bend) + 0.5 * hidden * (1.0 - bend * bend) * inner


def unit_back_kernel(grad_ref, weight_ref, hidden_ref, out_ref):
    d_act = mm_nt(grad_ref[...], weight_ref[...])
    out_ref[...] = (d_act * gelu_slope(hidden_ref[...])).astype(BF)


def unit_back(grad, weight, hidden):
    rows, depth = grad.shape
    units = weight.shape[0]
    size = min(512, units)
    tile = pl.BlockSpec((rows, size), lambda j: (0, j))
    return pl.pallas_call(
        unit_back_kernel,
        grid=(units // size,),
        in_specs=[
            pl.BlockSpec((rows, depth), lambda j: (0, 0)),
            pl.BlockSpec((size, depth), lambda j: (j, 0)),
            tile,
        ],
        out_specs=tile,
        out_shape=jax.ShapeDtypeStruct((rows, units), BF),
        compiler_params=pltpu.CompilerParams(vmem_limit_bytes=48 * 2**20),
        cost_estimate=BRIEF,
        name="unit_back",
    )(grad, weight, hidden)


def grad_kernel(pairs, *refs):
    total = sum(mm_tn(refs[2 * i][...], refs[2 * i + 1][...]) for i in range(pairs))
    at = 0
    for out_ref in refs[2 * pairs :]:
        out_ref[...] = total[:, at : at + out_ref.shape[1]].astype(BF)
        at += out_ref.shape[1]


def brief_grad(pairs, widths):
    rows = pairs[0][0].shape[1]
    size = min(256, rows)
    specs = []
    args = []
    for left, right in pairs:
        specs.append(pl.BlockSpec((left.shape[0], size), lambda i: (0, i)))
        specs.append(pl.BlockSpec(right.shape, lambda i: (0, 0)))
        args += [left, right]
    return pl.pallas_call(
        functools.partial(grad_kernel, len(pairs)),
        grid=(rows // size,),
        in_specs=specs,
        out_specs=[pl.BlockSpec((size, width), lambda i: (i, 0)) for width in widths],
        out_shape=[jax.ShapeDtypeStruct((rows, width), BF) for width in widths],
        compiler_params=pltpu.CompilerParams(vmem_limit_bytes=52 * 2**20),
        cost_estimate=BRIEF,
        name="brief_grad",
    )(*args)


def norm_kernel(half, x_ref, gain_ref, shift_ref, out_ref):
    wide = x_ref[...].astype(F32)
    mean = jnp.mean(wide, axis=1, keepdims=True)
    centred = wide - mean
    inv = lax.rsqrt(jnp.mean(centred * centred, axis=1, keepdims=True) + EPSILON)
    out_ref[...] = (centred * inv * gain_ref[...] + shift_ref[...]).astype(BF)


def norm_rows(tokens, half, length, gain, shift):
    width = tokens.shape[1]
    size = 256
    steps = length // size
    vector = pl.BlockSpec((1, width), lambda i, *_: (0, 0))
    return pl.pallas_call(
        norm_kernel,
        grid_spec=pltpu.PrefetchScalarGridSpec(
            num_scalar_prefetch=1,
            grid=(steps,),
            in_specs=[
                pl.BlockSpec((size, width), lambda i, at: (at[0] * steps + i, 0)),
                vector,
                vector,
            ],
            out_specs=pl.BlockSpec((size, width), lambda i, at: (i, 0)),
        ),
        out_shape=jax.ShapeDtypeStruct((length, width), BF),
        compiler_params=pltpu.CompilerParams(vmem_limit_bytes=40 * 2**20),
        cost_estimate=BRIEF,
        name="norm_rows",
    )(half[None], tokens, gain[None], shift[None])


def norm_back_kernel(at, kept_ref, near_ref, far_ref, *refs):
    if len(refs) == 6:
        standard_ref, inv_ref, add_ref, gain_ref, out_ref, sums_ref = refs
        standard = standard_ref[...]
        inv = inv_ref[...]
        add = add_ref[...].astype(F32)
    else:
        x_ref, gain_ref, out_ref, sums_ref = refs
        wide = x_ref[...].astype(F32)
        centred = wide - jnp.mean(wide, axis=1, keepdims=True)
        inv = lax.rsqrt(jnp.mean(centred * centred, axis=1, keepdims=True) + EPSILON)
        standard = centred * inv
        add = None
    grad = kept_ref[...].astype(F32) + near_ref[...].astype(F32) + far_ref[...].astype(F32)
    scaled = grad * gain_ref[...]
    moment = jnp.mean(scaled * standard, axis=1, keepdims=True)
    result = inv * (scaled - jnp.mean(scaled, axis=1, keepdims=True) - standard * moment)
    if add is not None:
        result = add + result
    out_ref[...] = result.astype(BF)

    @pl.when(pl.program_id(0) == 0)
    def _():
        sums_ref[...] = jnp.zeros_like(sums_ref)

    sums_ref[0:1, :] += jnp.sum(grad * standard, axis=0, keepdims=True)
    sums_ref[1:2, :] += jnp.sum(grad, axis=0, keepdims=True)
    if add is not None:
        sums_ref[2:3, :] += jnp.sum(result.astype(BF).astype(F32), axis=0, keepdims=True)
        sums_ref[3:4, :] += jnp.sum(add, axis=0, keepdims=True)


def norm_back(kept, mine, near, far, gain, *inputs, token_block=None):
    rows, width = near.shape
    size = rows // 2 if (rows // 2) % 16 == 0 else rows
    steps = rows // size
    if token_block is None:
        token_block = jnp.zeros_like(mine)
    tile = pl.BlockSpec((size, width), lambda i, at: (i, 0))
    specs = [pl.BlockSpec((size, width), lambda i, at: (at[0] * steps + i, 0)), tile, tile]
    if len(inputs) == 3:
        specs += [tile, pl.BlockSpec((size, 1), lambda i, at: (i, 0)), tile]
    else:
        specs += [pl.BlockSpec((size, width), lambda i, at: (at[1] * steps + i, 0))]
    specs.append(pl.BlockSpec((1, width), lambda i, at: (0, 0)))
    return pl.pallas_call(
        norm_back_kernel,
        grid_spec=pltpu.PrefetchScalarGridSpec(
            num_scalar_prefetch=1,
            grid=(steps,),
            in_specs=specs,
            out_specs=[tile, pl.BlockSpec((8, width), lambda i, at: (0, 0))],
        ),
        out_shape=[
            jax.ShapeDtypeStruct((rows, width), BF),
            jax.ShapeDtypeStruct((8, width), F32),
        ],
        compiler_params=pltpu.CompilerParams(vmem_limit_bytes=48 * 2**20),
        cost_estimate=BRIEF,
        name="norm_back",
    )(jnp.stack((mine, token_block)), kept, near, far, *inputs, gain[None])


def row_sums_kernel(*refs):
    refs[-1][...] = sum(jnp.sum(r[...].astype(F32), axis=0, keepdims=True) for r in refs[:-1])


def row_sums(*arrays):
    width = arrays[0].shape[1]
    size = 512 if width % 512 == 0 else width
    return pl.pallas_call(
        row_sums_kernel,
        grid=(width // size,),
        in_specs=[pl.BlockSpec((array.shape[0], size), lambda i: (0, i)) for array in arrays],
        out_specs=pl.BlockSpec((1, size), lambda i: (0, i)),
        out_shape=jax.ShapeDtypeStruct((1, width), F32),
        compiler_params=pltpu.CompilerParams(vmem_limit_bytes=40 * 2**20),
        cost_estimate=BRIEF,
        name="row_sums",
    )(*arrays)[0]


def gather_kernel(x_ref, pos_ref, out_ref):
    wanted = pos_ref[0]
    total = jnp.zeros(out_ref.shape, F32)
    for start in range(0, x_ref.shape[0], BK):
        here = start + lax.broadcasted_iota(jnp.int32, (BK, wanted.shape[1]), 0)
        total = total + mm_tn((here == wanted).astype(BF), x_ref[start : start + BK, :])
    out_ref[...] = total.astype(BF)


def gather_slots(values, positions, capacity, length):
    rows = positions.shape[0]
    width = values.shape[1]
    return pl.pallas_call(
        gather_kernel,
        grid=(rows,),
        in_specs=[
            pl.BlockSpec((length, width), lambda r: (r, 0)),
            pl.BlockSpec((1, 1, capacity), lambda r: (r, 0, 0)),
        ],
        out_specs=pl.BlockSpec((capacity, width), lambda r: (r, 0)),
        out_shape=jax.ShapeDtypeStruct((rows * capacity, width), BF),
        compiler_params=pltpu.CompilerParams(vmem_limit_bytes=40 * 2**20),
        cost_estimate=BRIEF,
        name="gather_slots",
    )(values, positions[:, None, :capacity])


def place_kernel(wide, at, slots_ref, slot_ref, base_ref, *refs):
    out_ref = refs[-1]
    capacity = slots_ref.shape[0]
    size, width = out_ref.shape
    here = lax.broadcasted_iota(jnp.int32, (capacity, size), 0)
    one = (here == slot_ref[0]).astype(BF)
    hit = mm_tn(one, jnp.ones((capacity, width), BF))
    result = jnp.where(hit > 0.5, mm_tn(one, slots_ref[...]), base_ref[...].astype(F32))
    if wide:
        result = result + refs[0][...].astype(F32)
    out_ref[...] = result.astype(out_ref.dtype)


def place_tokens(slot_values, slot, base, column, addend=None):
    rows, length = slot.shape
    width = slot_values.shape[1]
    capacity = slot_values.shape[0] // rows
    size = 512
    steps = length // size
    token_spec = pl.BlockSpec((size, width), lambda r, i, *_: (r * steps + i, 0))
    if base.shape[1] % 128 == 0 and width % 128 == 0:
        base_spec = pl.BlockSpec((size, width), lambda r, i, at: (r * steps + i, at[0]))
    else:
        base = lax.dynamic_slice_in_dim(base, column * width, width, 1)
        base_spec = token_spec
    out_type = BF if addend is None else F32
    extra = [] if addend is None else [addend]
    return pl.pallas_call(
        functools.partial(place_kernel, addend is not None),
        grid_spec=pltpu.PrefetchScalarGridSpec(
            num_scalar_prefetch=1,
            grid=(rows, steps),
            in_specs=[
                pl.BlockSpec((capacity, width), lambda r, i, *_: (r, 0)),
                pl.BlockSpec((1, 1, size), lambda r, i, *_: (r, 0, i)),
                base_spec,
            ]
            + [token_spec] * len(extra),
            out_specs=token_spec,
        ),
        out_shape=jax.ShapeDtypeStruct((rows * length, width), out_type),
        compiler_params=pltpu.CompilerParams(vmem_limit_bytes=40 * 2**20),
        cost_estimate=BRIEF,
        name="place_tokens",
    )(column[None], slot_values, slot[:, None, :], base, *extra)


def split_heads(pairs, heads):
    lane = lax.broadcasted_iota(jnp.int32, (pairs.shape[0], 128), 1)
    out = []
    for pair in range(heads // 2):
        part = pairs[:, 128 * pair : 128 * pair + 128]
        zero = jnp.zeros_like(part)
        out += [jnp.where(lane < 64, part, zero), jnp.where(lane < 64, zero, part)]
    return out


def merge_heads(parts, block):
    row = lax.broadcasted_iota(jnp.int32, (128, block), 0)
    return [
        jnp.where(row < 64, parts[2 * pair], parts[2 * pair + 1])
        for pair in range(len(parts) // 2)
    ]


def unpack(heads, packed_ref, q_all, k_all, v_all):
    lane = lax.broadcasted_iota(jnp.int32, (packed_ref.shape[0], 128), 1)
    for pair in range(heads // 2):
        lanes = slice(128 * pair, 128 * pair + 128)
        part = [packed_ref[:, 384 * pair + 128 * i : 384 * pair + 128 * i + 128] for i in range(3)]
        q_all[:, lanes] = jnp.where(lane < 64, part[0], part[1])
        keys = jnp.where(lane < 64, part[2], part[0])
        k_all[:, lanes] = pltpu.roll(keys.astype(F32), 64, 1).astype(BF)
        v_all[:, lanes] = jnp.where(lane < 64, part[1], part[2])


def attend_kernel(
    heads,
    first,
    last,
    near,
    packed_ref,
    lo_ref,
    hi_ref,
    o_ref,
    low_ref,
    lse_ref,
    q_ref,
    q_all,
    k_all,
    v_all,
):
    block = pl.program_id(0)

    @pl.when(block == 0)
    def _():
        unpack(heads, packed_ref, q_all, k_all, v_all)

    lo = lo_ref[...]
    hi = hi_ref[...]

    def pick_step(window, total):
        start = pl.multiple_of(window * BK, BK)
        here = start + lax.broadcasted_iota(jnp.int32, (BK, BQ), 0)
        return total + mm_tn((here == hi).astype(BF), q_all[pl.ds(start, BK), :])

    picked = lax.fori_loop(near[block], last[block], pick_step, jnp.zeros(q_ref.shape, F32))
    picked = picked.astype(BF)
    q_ref[...] = picked
    queries = split_heads(picked * jnp.asarray(SCALE, BF), heads)

    def step(key_block, carried):
        start = pl.multiple_of(key_block * BK, BK)
        key_pos = start + lax.broadcasted_iota(jnp.int32, (BK, BQ), 0)
        allowed = (key_pos >= lo) & (key_pos <= hi)
        raw = [
            mm_nt(k_all[pl.ds(start, BK), 128 * (h // 2) : 128 * (h // 2) + 128], queries[h])
            for h in range(heads)
        ]
        out = []
        for h in range(heads):
            values = v_all[pl.ds(start, BK), 128 * (h // 2) : 128 * (h // 2) + 128]
            top, total, mixed = carried[3 * h : 3 * h + 3]
            scores = jnp.where(allowed, raw[h], MASKED)
            new_top = jnp.maximum(top, jnp.max(scores, axis=0, keepdims=True))
            weights = jnp.exp(scores - new_top)
            fade = jnp.exp(top - new_top)
            total = total * fade + jnp.sum(weights, axis=0, keepdims=True)
            mixed = mixed * fade + mm_tn(values, weights.astype(BF))
            out += [new_top, total, mixed]
        return tuple(out)

    init = (
        jnp.full((1, BQ), MASKED, F32),
        jnp.zeros((1, BQ), F32),
        jnp.zeros((128, BQ), F32),
    ) * heads
    done = lax.fori_loop(first[block], last[block], step, init)
    merged = merge_heads([done[3 * h + 2] / done[3 * h + 1] for h in range(heads)], BQ)
    for pair in range(heads // 2):
        part = merged[pair].T
        o_ref[:, 128 * pair : 128 * pair + 128] = part
        low_ref[:, 128 * pair : 128 * pair + 128] = part.astype(BF)
    row = lax.broadcasted_iota(jnp.int32, (8, BQ), 0)
    lse = jnp.zeros((8, BQ), F32)
    for h in range(heads):
        lse = jnp.where(row == h, done[3 * h] + jnp.log(done[3 * h + 1]), lse)
    lse_ref[...] = lse


def attend(packed, lo, hi, bounds):
    count = hi.shape[1]
    length = packed.shape[0]
    width = packed.shape[1] // 3
    heads = width // HD
    row_spec = pl.BlockSpec((1, BQ), lambda i, *_: (0, i))
    block_spec = pl.BlockSpec((BQ, width), lambda i, *_: (i, 0))
    spec = pltpu.PrefetchScalarGridSpec(
        num_scalar_prefetch=3,
        grid=(count // BQ,),
        in_specs=[
            pl.BlockSpec((length, 3 * width), lambda i, *_: (0, 0)),
            row_spec,
            row_spec,
        ],
        out_specs=[
            block_spec,
            block_spec,
            pl.BlockSpec((8, BQ), lambda i, *_: (0, i)),
            block_spec,
        ],
        scratch_shapes=[pltpu.VMEM((length, width), BF)] * 3,
    )
    return pl.pallas_call(
        functools.partial(attend_kernel, heads),
        grid_spec=spec,
        out_shape=[
            jax.ShapeDtypeStruct((count, width), F32),
            jax.ShapeDtypeStruct((count, width), BF),
            jax.ShapeDtypeStruct((8, count), F32),
            jax.ShapeDtypeStruct((count, width), BF),
        ],
        compiler_params=pltpu.CompilerParams(vmem_limit_bytes=48 * 2**20),
        cost_estimate=BRIEF,
        name="attend",
    )(*bounds, packed, lo, hi)


def attend_back_kernel(
    heads,
    first,
    last,
    near,
    packed_ref,
    q_ref,
    g_ref,
    o_ref,
    lse_ref,
    lo_ref,
    hi_ref,
    *refs,
):
    out_ref, q_all, k_all, v_all, dq_sum, dk_sum, dv_sum = refs[-7:]
    count, width = q_ref.shape
    unpack(heads, packed_ref, q_all, k_all, v_all)
    dq_sum[...] = jnp.zeros_like(dq_sum)
    dk_sum[...] = jnp.zeros_like(dk_sum)
    dv_sum[...] = jnp.zeros_like(dv_sum)
    head_of = lax.broadcasted_iota(jnp.int32, (8, width), 1) // HD
    picks = (head_of == lax.broadcasted_iota(jnp.int32, (8, width), 0)).astype(F32)

    def query_step(block, _):
        at = pl.multiple_of(block * BQ, BQ)
        queries = split_heads(q_ref[pl.ds(at, BQ), :] * jnp.asarray(SCALE, BF), heads)
        grad = g_ref[pl.ds(at, BQ), :]
        grads = split_heads(grad, heads)
        lo = lo_ref[:, pl.ds(at, BQ)]
        hi = hi_ref[:, pl.ds(at, BQ)]
        delta = lax.dot_general(
            picks,
            grad.astype(F32) * o_ref[pl.ds(at, BQ), :],
            NT,
            precision=lax.Precision.HIGHEST,
            preferred_element_type=F32,
        )

        def key_step(key_block, carried):
            start = pl.multiple_of(key_block * BK, BK)
            key_pos = start + lax.broadcasted_iota(jnp.int32, (BK, BQ), 0)
            allowed = (key_pos >= lo) & (key_pos <= hi)
            out = []
            for pair in range(heads // 2):
                lanes = slice(128 * pair, 128 * pair + 128)
                keys = k_all[pl.ds(start, BK), lanes]
                values = v_all[pl.ds(start, BK), lanes]
                dk = dk_sum[pl.ds(start, BK), lanes]
                dv = dv_sum[pl.ds(start, BK), lanes]
                for h in (2 * pair, 2 * pair + 1):
                    scores = mm_nt(keys, queries[h])
                    shares = jnp.exp(
                        jnp.where(allowed, scores, MASKED) - lse_ref[h : h + 1, pl.ds(at, BQ)]
                    )
                    d_shares = mm_nt(values, grads[h])
                    d_scores = (shares * (d_shares - delta[h : h + 1, :])).astype(BF)
                    dv = dv + mm(shares.astype(BF), grads[h])
                    dk = dk + mm(d_scores, queries[h])
                    out.append(carried[h] + mm_tn(keys, d_scores))
                dk_sum[pl.ds(start, BK), lanes] = dk
                dv_sum[pl.ds(start, BK), lanes] = dv
            return tuple(out)

        done = lax.fori_loop(
            first[block], last[block], key_step, (jnp.zeros((128, BQ), F32),) * heads
        )
        d_queries = [(part.T * SCALE).astype(BF) for part in merge_heads(done, BQ)]

        def place_step(window, _):
            start = pl.multiple_of(window * BK, BK)
            here = start + lax.broadcasted_iota(jnp.int32, (BK, BQ), 0)
            one = (here == hi).astype(BF)
            for pair in range(heads // 2):
                lanes = slice(128 * pair, 128 * pair + 128)
                dq_sum[pl.ds(start, BK), lanes] += mm(one, d_queries[pair])
            return 0

        lax.fori_loop(near[block], last[block], place_step, 0)
        return 0

    lax.fori_loop(0, count // BQ, query_step, 0)
    lane = lax.broadcasted_iota(jnp.int32, (out_ref.shape[0], 128), 1)
    for pair in range(heads // 2):
        lanes = slice(128 * pair, 128 * pair + 128)
        dq = dq_sum[:, lanes]
        dk = pltpu.roll(dk_sum[:, lanes], 64, 1)
        dv = dv_sum[:, lanes]
        merged = (
            jnp.where(lane < 64, dq, dk),
            jnp.where(lane < 64, dv, dq),
            jnp.where(lane < 64, dk, dv),
        )
        for i, part in enumerate(merged):
            out_ref[:, 384 * pair + 128 * i : 384 * pair + 128 * i + 128] = part.astype(BF)


def attend_back(packed, queries, grads, column, mixed, lse, lo, hi, bounds, sets, joined):
    count, width = queries.shape
    length = packed.shape[0]
    heads = width // HD
    query_spec = pl.BlockSpec((count, width), lambda i, *_: (0, 0))
    grad_spec = pl.BlockSpec((count, width), lambda i, *_: (0, column))
    packed_spec = pl.BlockSpec((length, 3 * width), lambda i, *_: (0, 0))
    row_spec = pl.BlockSpec((1, count), lambda i, *_: (0, 0))
    spec = pltpu.PrefetchScalarGridSpec(
        num_scalar_prefetch=3,
        grid=(1,),
        in_specs=[
            packed_spec,
            query_spec,
            grad_spec,
            query_spec,
            pl.BlockSpec((8, count), lambda i, *_: (0, 0)),
            row_spec,
            row_spec,
        ]
        + [pl.BlockSpec(memory_space=pl.ANY)] * (joined is not None),
        out_specs=pl.BlockSpec((length, 3 * width), lambda i, *_: (0, column)),
        scratch_shapes=[pltpu.VMEM((length, width), BF)] * 3
        + [pltpu.VMEM((length, width), F32)] * 3,
    )
    return pl.pallas_call(
        functools.partial(attend_back_kernel, heads),
        grid_spec=spec,
        out_shape=jax.ShapeDtypeStruct((length, 3 * width * sets), BF),
        input_output_aliases={} if joined is None else {10: 0},
        compiler_params=pltpu.CompilerParams(vmem_limit_bytes=58 * 2**20),
        cost_estimate=BRIEF,
        name="attend_back",
    )(*bounds, packed, queries, grads, mixed, lse, lo, hi, *([] if joined is None else [joined]))


def swap_halves(value):
    return lax.ppermute(value, "half", [(0, 1), (1, 0)])


def swap_by_gather(value):
    rows = value.shape[0]
    pair = lax.all_gather(value, "half", axis=0, tiled=True)
    return lax.dynamic_slice_in_dim(pair, (1 - lax.axis_index("half")) * rows, rows, 0)


def exchange(value, bit, axis="tp"):
    return lax.ppermute(value, axis, [(i, i ^ bit) for i in range(lax.axis_size(axis))])


def gather_near(value):
    bit = 1
    while bit < lax.axis_size("tp") // 2:
        value = jnp.concatenate((value, exchange(value, bit)), axis=0)
        bit *= 2
    return value


def send_top(value):
    return exchange(value, lax.axis_size("tp") // 2)


def fold_parts(value, natural, *beside, bit=None):
    bit = lax.axis_size("tp") // 4 if bit is None else bit
    place = lax.axis_index("tp")
    while True:
        rows = value.shape[0] // 2
        mine = (place // bit) % 2 if natural else jnp.zeros_like(place)
        sent = lax.dynamic_slice_in_dim(value, (1 - mine) * rows, rows, 0) if natural else value[rows:]
        received = exchange(sent.astype(BF), bit)
        received = tie(received, *beside) if beside else received
        if bit == 1:
            return value, mine, received
        value = add_parts(value, mine, received)
        bit //= 2


def add_parts(kept, mine, received):
    rows = received.shape[0]
    kept = lax.dynamic_slice_in_dim(kept, mine * rows, rows, 0)
    return kept.astype(F32) + received.astype(F32)


def fold_tp(value, *beside):
    return add_parts(*fold_parts(value, False, *beside))


def fold_natural(value):
    return add_parts(*fold_parts(value, True))


def natural_halves(value):
    rows = value.shape[0] // 2
    top = lax.axis_index("tp") // (lax.axis_size("tp") // 2)
    return (
        lax.dynamic_slice_in_dim(value, top * rows, rows, 0),
        lax.dynamic_slice_in_dim(value, (1 - top) * rows, rows, 0),
    )


def relative_rows(value):
    count = lax.axis_size("tp")
    size = value.shape[0] // count
    place = lax.axis_index("tp")
    blocks = [
        lax.dynamic_slice_in_dim(value, (place ^ k) * size, size, 0) for k in range(count)
    ]
    middle = count // 2
    return jnp.concatenate(blocks[:middle], axis=0), jnp.concatenate(blocks[middle:], axis=0)


def both(parts):
    return jnp.concatenate(parts, axis=0)


def own_dp_part(weight):
    part = weight.shape[0] // lax.axis_size("dp")
    return lax.dynamic_slice_in_dim(weight, lax.axis_index("dp") * part, part, 0)


def spread_first(part):
    return exchange(part, 1, "dp"), exchange(part, 2, "dp")


def spread_second(part, first):
    count = lax.axis_size("dp")
    one, two = first
    middle = part.shape[0] // 2
    blocks = [(0, 0, part), (1, 0, one), (2, 0, two)]
    blocks.append((3, 0, exchange(two[:middle], 1, "dp")))
    blocks.append((3, middle, exchange(one[middle:], 2, "dp")))
    bit = 4
    while bit < count:
        blocks = blocks + [(k + bit, at, exchange(block, bit, "dp")) for k, at, block in blocks]
        bit *= 2
    return blocks


def whole_parts(blocks):
    parts = {}
    for k, _, block in blocks:
        parts.setdefault(k, []).append(block)
    return [jnp.concatenate(parts[k], axis=0) for k in range(len(parts))]


def assemble(buffer, blocks, row, column):
    member = lax.axis_index("dp")
    size = buffer.shape[0] - row
    part = size // lax.axis_size("dp")
    for k, offset, block in blocks:
        start = row + (member ^ k) * part + offset
        buffer = lax.dynamic_update_slice(buffer, block, (start, column))
    return buffer


def sum_over_dp(grad, dimension):
    return lax.psum_scatter(grad.astype(BF), "dp", scatter_dimension=dimension, tiled=True)


ALL = ("half", "tp")


def running_count(flags):
    rows, length = flags.shape
    chunk = 128
    tiles = flags.reshape(rows, length // chunk, chunk)
    ones = (
        lax.broadcasted_iota(jnp.int32, (chunk, chunk), 0)
        <= lax.broadcasted_iota(jnp.int32, (chunk, chunk), 1)
    ).astype(BF)
    inside = jnp.einsum("rtc,cd->rtd", tiles.astype(BF), ones, preferred_element_type=F32)
    totals = jnp.sum(tiles, axis=2)
    tile_count = length // chunk
    earlier = (
        lax.broadcasted_iota(jnp.int32, (tile_count, tile_count), 0)
        < lax.broadcasted_iota(jnp.int32, (tile_count, tile_count), 1)
    ).astype(F32)
    before = jnp.sum(totals[:, :, None] * earlier[None], axis=1)
    return (inside + before[:, :, None]).reshape(rows, length)


def prepare(
    tokens,
    segment_ids,
    exit_layer,
    norm1_gain,
    norm1_shift,
    w_qkv,
    b_qv,
    w_out,
    b_out,
    norm2_gain,
    norm2_shift,
    w_up,
    b_up,
    w_down,
    b_down,
    cotangent,
):
    half = lax.axis_index("half")
    rows, length = segment_ids.shape
    own_heads = b_qv.shape[0] // (2 * HD)

    far_qkv_part = swap_halves(own_dp_part(w_qkv))
    far_out_part = swap_halves(own_dp_part(w_out))
    far_vectors = swap_halves(jnp.concatenate((b_qv, b_up, b_out, b_down)))

    active = exit_layer > LAYER
    most = jnp.max(jnp.sum(active.astype(F32), axis=1)) * jnp.ones((8, 128), F32)
    bit = 1
    while bit < lax.axis_size("dp"):
        most = jnp.maximum(most, exchange(most, bit, "dp"))
        bit *= 2

    normed1 = norm_rows(
        tokens, half, length, norm1_gain.astype(F32), norm1_shift.astype(F32)
    )
    own_packed = (mm(normed1, w_qkv) + qkv_bias(b_qv)).astype(BF)

    running = running_count(active.astype(F32)).astype(jnp.int32)
    slot = jnp.where(active, running - 1, -1)
    slots = lax.broadcasted_iota(jnp.int32, (1, length, 1), 1)
    positions = jnp.sum((running[:, None, :] <= slots).astype(jnp.int32), axis=2)
    own_positions = lax.dynamic_index_in_dim(positions, half, 0, keepdims=False)
    own_docs = lax.dynamic_index_in_dim(segment_ids, half, 0, keepdims=False)
    doc_numbers = jnp.arange(DOCS, dtype=jnp.int32)[:, None]
    doc_starts = jnp.sum((own_docs[None, :] < doc_numbers).astype(jnp.int32), axis=1, keepdims=True)
    hi = jnp.minimum(own_positions, length - 1)
    lo = jnp.max(jnp.where(doc_starts <= hi[None, :], doc_starts, 0), axis=0)
    prepared = (far_qkv_part, far_out_part, far_vectors, normed1, own_packed)
    prepared += (slot, positions, own_positions, lo, hi)
    return most[0, 0], prepared


def qkv_bias(bias):
    pairs = bias.astype(F32).reshape(-1, 2, HD)
    zero = jnp.zeros_like(pairs[:, 0])
    return jnp.stack((pairs[:, 0], zero, pairs[:, 1]), axis=1).reshape(-1)


def layer(
    capacity,
    prepared,
    tokens,
    segment_ids,
    exit_layer,
    norm1_gain,
    norm1_shift,
    w_qkv,
    b_qv,
    w_out,
    b_out,
    norm2_gain,
    norm2_shift,
    w_up,
    b_up,
    w_down,
    b_down,
    cotangent,
):
    far_qkv_part, far_out_part, far_vectors, normed1, own_packed = prepared[:5]
    slot, positions, own_positions, lo, hi = prepared[5:]
    n_tp = lax.axis_size("tp")
    half = lax.axis_index("half")
    place = lax.axis_index("tp")
    rows, length = segment_ids.shape
    width = tokens.shape[1]
    own_width = cotangent.shape[1]
    device = half * n_tp + place
    own_heads = b_qv.shape[0] // (2 * HD)
    units = w_up.shape[1]
    cap_all = -(-capacity // BQ) * BQ
    cap_part = capacity // n_tp
    part = length // n_tp
    gain1 = norm1_gain.astype(F32)

    lo = lo[:cap_all]
    hi = hi[:cap_all]
    bounds = (lo[::BQ] // BK, hi[BQ - 1 :: BQ] // BK + 1, hi[::BQ] // BK)
    lo = lo[None]
    hi = hi[None]

    size = b_qv.shape[0]
    far_b_qv = far_vectors[:size]
    far_b_up = far_vectors[size : size + units]
    far_b_out = far_vectors[size + units : size + units + own_width]
    far_b_down = far_vectors[size + units + own_width :]

    def share_of_bias(own, far):
        bias = jnp.zeros((width,), F32)
        bias = lax.dynamic_update_slice(bias, own.astype(F32), (device * own_width,))
        other = (1 - half) * n_tp + place
        return lax.dynamic_update_slice(bias, far.astype(F32), (other * own_width,))

    far_qkv_first = spread_first(far_qkv_part)
    far_out = lax.all_gather(far_out_part, "dp", axis=0, tiled=True)
    own_cot = gather_slots(cotangent, positions, capacity, length)
    cot = lax.all_to_all(own_cot, ALL, split_axis=0, concat_axis=1, tiled=True)

    if own_heads % 2:
        far_qkv_blocks = spread_second(far_qkv_part, far_qkv_first)
        far_qkv = assemble(jnp.zeros_like(w_qkv), far_qkv_blocks, 0, 0)
        far_packed = (mm(normed1, far_qkv) + qkv_bias(far_b_qv)).astype(BF)
        packs = [jnp.concatenate((own_packed, far_packed), axis=1)]
        far_up_part = swap_halves(own_dp_part(w_up))
        kept = [attend(packs[0], lo, hi, bounds)]
    else:
        own_kept = attend(own_packed, lo, hi, bounds)
        far_out, far_qkv_first, *own_kept = lax.optimization_barrier(
            (far_out, far_qkv_first, *own_kept)
        )
        far_qkv_blocks = spread_second(far_qkv_part, far_qkv_first)
        far_up_part = swap_by_gather(tie(own_dp_part(w_up), far_out))
        far_packed = brief_by_parts(normed1, whole_parts(far_qkv_blocks), qkv_bias(far_b_qv))
        packs = [own_packed, far_packed]
        kept = [own_kept, attend(far_packed, lo, hi, bounds)]
    far_up_part, cot, head_out = lax.optimization_barrier(
        (far_up_part, cot, jnp.concatenate([item[1] for item in kept], axis=1))
    )
    far_down_part = swap_by_gather(tie(own_dp_part(w_down), far_up_part))
    far_up_first = spread_first(far_up_part)

    out_weight = jnp.concatenate((w_out, far_out), axis=0)
    head_out = head_out[:capacity]
    near_rows, far_rows = natural_halves(head_out)
    out_bias = share_of_bias(b_out, far_b_out)
    far_branch = fold_natural((mm(far_rows, out_weight) + out_bias).astype(BF)).astype(BF)
    near_branch = fold_natural((mm(near_rows, out_weight) + out_bias).astype(BF))
    recv_branch = send_top(far_branch)
    part_positions = lax.dynamic_slice_in_dim(own_positions, place * cap_part, cap_part)
    part_pick = (
        part_positions[:, None] == lax.broadcasted_iota(jnp.int32, (1, length), 1)
    ).astype(BF)
    own_inputs = lax.dynamic_slice_in_dim(tokens, half * length, length, 0)
    part_inputs = mm(tie(part_pick, far_branch), own_inputs).astype(BF)
    qkv_weight = assemble(
        jnp.pad(tie(w_qkv, far_branch), ((0, 0), (0, w_qkv.shape[1]))),
        far_qkv_blocks,
        0,
        w_qkv.shape[1],
    )
    up_weight = jnp.pad(tie(w_up, far_branch), ((0, 0), (0, units)))
    near_d_ffn = gather_near(cot)
    far_up_first, part_inputs = lax.optimization_barrier((far_up_first, part_inputs))
    far_up_blocks = spread_second(far_up_part, far_up_first)
    up_weight = assemble(up_weight, far_up_blocks, 0, units)
    down_weight = jnp.pad(tie(w_down, far_branch), ((0, units), (0, 0)))
    recv_branch, near_branch, up_weight, qkv_weight, down_weight = lax.optimization_barrier(
        (recv_branch, near_branch, up_weight, qkv_weight, down_weight)
    )
    residual = part_inputs.astype(F32) + near_branch + recv_branch.astype(F32)
    mean2 = jnp.mean(residual, axis=1, keepdims=True)
    inv2 = lax.rsqrt(jnp.mean(jnp.square(residual - mean2), axis=1, keepdims=True) + EPSILON)
    standard2 = (residual - mean2) * inv2
    gain2 = norm2_gain.astype(F32)
    part_normed2 = (standard2 * gain2 + norm2_shift.astype(F32)).astype(BF)
    far_down_first = spread_first(far_down_part)
    near_normed2 = gather_near(part_normed2)
    far_normed2 = send_top(part_normed2)
    up_bias = jnp.concatenate((b_up, far_b_up)).astype(F32)

    def forward(part_in):
        hidden = mm(part_in, up_weight) + up_bias
        return jax.nn.gelu(hidden, approximate=True).astype(BF), hidden

    near_act, near_hidden = forward(near_normed2)
    far_normed2, near_act, far_down_first = lax.optimization_barrier(
        (far_normed2, near_act, far_down_first)
    )
    far_cot = send_top(tie(cot, far_normed2))
    far_normed2 = gather_near(far_normed2)
    far_act, far_hidden = forward(far_normed2)
    down_weight = assemble(
        down_weight, spread_second(far_down_part, far_down_first), units, 0
    )
    down_weight, far_act, far_cot = lax.optimization_barrier((down_weight, far_act, far_cot))
    far_d_ffn = gather_near(far_cot)
    far_d_hidden = (mm_nt(far_d_ffn, down_weight) * gelu_slope(far_hidden)).astype(BF)
    down_bias = share_of_bias(b_down, far_b_down)
    far_d_normed2 = mm_nt(far_d_hidden, up_weight).astype(BF)
    far_ffn = (mm(tie(far_act, far_d_normed2), down_weight) + down_bias).astype(BF)
    far_d_normed2 = fold_tp(far_d_normed2, far_ffn).astype(BF)
    recv_d_normed2 = send_top(far_d_normed2)
    (grad_down,) = brief_grad(
        ((tie(near_act, far_d_normed2), near_d_ffn), (far_act, far_d_ffn)), (width,)
    )
    near_d_hidden = unit_back(tie(near_d_ffn, grad_down), down_weight, near_hidden)
    grad_down_sum = sum_over_dp(grad_down.reshape(2, units, width), 2)
    near_d_normed2 = brief_mm(near_d_hidden, up_weight, None, True)
    recv_d_normed2, near_d_normed2, grad_down = lax.optimization_barrier(
        (recv_d_normed2, near_d_normed2, grad_down)
    )
    near_d_normed2 = fold_parts(near_d_normed2, False)

    d_branch_part, sums2 = norm_back(*near_d_normed2, recv_d_normed2, gain2, standard2, inv2, cot)
    far_d_branch = send_top(d_branch_part)
    near_d_branch = gather_near(d_branch_part)
    near_d_heads = brief_mm(near_d_branch, out_weight, None, True)
    near_ffn = brief_mm(tie(near_act, near_d_heads), down_weight, down_bias)
    (grad_up,) = brief_grad(
        ((tie(near_normed2, near_ffn), near_d_hidden), (far_normed2, far_d_hidden)), (2 * units,)
    )
    far_d_branch, grad_up, near_ffn = lax.optimization_barrier((far_d_branch, grad_up, near_ffn))
    far_ffn = fold_tp(tie(far_ffn, far_d_branch)).astype(BF)
    near_ffn = fold_tp(tie(near_ffn, far_d_branch))
    recv_ffn = send_top(far_ffn)
    far_d_branch = gather_near(far_d_branch)
    d_heads = both((near_d_heads, mm_nt(far_d_branch, out_weight).astype(BF)))
    d_heads = jnp.pad(both(relative_rows(d_heads)), ((0, cap_all - capacity), (0, 0)))
    d_heads, grad_down = lax.optimization_barrier((d_heads, grad_down_sum))
    grad_up = sum_over_dp(tie(grad_up, grad_down), 0)
    far_swap_down = swap_halves(grad_down[1])
    d_residual_slots = lax.all_to_all(
        tie(d_branch_part, d_heads), ALL, split_axis=1, concat_axis=0, tiled=True
    )

    def back(at, joined):
        item = kept[at]
        return attend_back(
            packs[at], item[3], d_heads, at, item[0], item[2], lo, hi, bounds, len(packs), joined
        )

    d_pack = back(0, None)
    head_rows = relative_rows(head_out)
    (grad_out,) = brief_grad(
        ((tie(head_rows[0], d_pack), near_d_branch), (head_rows[1], far_d_branch)), (width,)
    )
    d_pack, grad_out, d_residual_slots = lax.optimization_barrier(
        (d_pack, grad_out, d_residual_slots)
    )
    if len(packs) == 2:
        d_pack = back(1, d_pack)
    d_pack, recv_ffn, far_swap_down = lax.optimization_barrier((d_pack, recv_ffn, far_swap_down))
    out_part = (residual + near_ffn + recv_ffn.astype(F32)).astype(BF)
    out_slots = lax.all_to_all(out_part, ALL, split_axis=1, concat_axis=0, tiled=True)
    d_pack = tie(d_pack, out_part)
    d_pack, grad_up = lax.optimization_barrier((d_pack, grad_up))
    far_swap_up = swap_halves(grad_up[:, units:])
    grad_out = sum_over_dp(tie(grad_out, grad_up), 1)
    top = place // (n_tp // 2)
    bit = n_tp // 4
    mine = (place // bit) % 2
    kept, sent = pair_mm(d_pack, qkv_weight, 2 * (1 - top) + mine, 2 * (1 - top) + 1 - mine)
    far_d_normed1 = brief_add(kept, exchange(sent, bit))
    if bit > 1:
        far_d_normed1 = add_parts(*fold_parts(far_d_normed1, True, bit=bit // 2)).astype(BF)
    recv_d_normed1 = send_top(far_d_normed1)
    near_pair = pair_mm(
        tie(d_pack, far_d_normed1), qkv_weight, 2 * top + mine, 2 * top + 1 - mine
    )
    near_received = exchange(near_pair[1], bit)
    near_d_normed1 = near_pair[0]
    qkv_width = w_qkv.shape[1]
    d_hidden_sums = row_sums(tie(near_d_hidden, far_d_normed1), far_d_hidden)
    d_pack_sums = row_sums(tie(d_pack, far_d_normed1))
    far_unit_sums = swap_halves(
        jnp.concatenate((d_pack_sums[qkv_width:], d_hidden_sums[units:]))
    )
    (raw_grad_qkv,) = brief_grad(((tie(normed1, near_d_normed1), d_pack),), (2 * qkv_width,))
    recv_d_normed1, raw_grad_qkv, grad_out, out_slots, far_swap_up, far_unit_sums = (
        lax.optimization_barrier(
            (recv_d_normed1, raw_grad_qkv, grad_out, out_slots, far_swap_up, far_unit_sums)
        )
    )
    grad_qkv = sum_over_dp(raw_grad_qkv, 0)
    near_d_normed1 = (near_d_normed1, jnp.zeros_like(place), near_received)
    if bit > 1:
        near_d_normed1 = fold_parts(add_parts(*near_d_normed1).astype(BF), True, bit=bit // 2)

    d_norm1_part, sums1 = norm_back(
        *near_d_normed1, recv_d_normed1, gain1, tokens, token_block=half * n_tp + place
    )
    spread = lax.all_to_all(
        jnp.concatenate((sums1[:2], sums2[:4])), ALL, split_axis=1, concat_axis=0, tiled=True
    )
    d_norm1_tokens = lax.all_to_all(
        tie(d_norm1_part, spread), ALL, split_axis=1, concat_axis=0, tiled=True
    )
    feature_sums = jnp.sum(spread.reshape(-1, 6, own_width), axis=0).reshape(-1)
    own_unit_sums = jnp.concatenate((d_pack_sums[:qkv_width], d_hidden_sums[:units]))
    summed = lax.psum(jnp.concatenate((feature_sums, own_unit_sums + far_unit_sums)), "dp")
    result = place_tokens(out_slots, tie(slot, d_norm1_part), tokens, device)
    d_norm1_tokens, result, summed = lax.optimization_barrier((d_norm1_tokens, result, summed))
    grad_qkv, grad_out = tie(grad_qkv, d_norm1_tokens), tie(grad_out, result)
    far_swap_qkv = swap_halves(grad_qkv[:, qkv_width:])
    d_inputs = place_tokens(
        d_residual_slots, slot, cotangent, jnp.zeros_like(device), d_norm1_tokens
    )

    def join(own, far):
        return own.astype(F32) + far.astype(F32)

    grad_down = join(grad_down[0], far_swap_down)
    grad_up = join(grad_up[:, :units], far_swap_up)
    out_rows = w_out.shape[0]
    grad_out = join(grad_out[:out_rows], swap_halves(grad_out[out_rows:]))
    grad_qkv = join(grad_qkv[:, :qkv_width], far_swap_qkv)

    feature_sums = summed[: 6 * own_width].reshape(6, own_width)
    unit_sums = summed[6 * own_width :]
    d_biases = unit_sums[:qkv_width].reshape(own_heads, 3, HD)
    d_biases = jnp.stack((d_biases[:, 0], d_biases[:, 2]), axis=1).reshape(-1)
    return (
        result,
        d_inputs,
        feature_sums[0],
        feature_sums[1],
        grad_qkv,
        d_biases,
        grad_out,
        feature_sums[4],
        feature_sums[2],
        feature_sums[3],
        grad_up,
        unit_sums[qkv_width:],
        grad_down,
        feature_sums[5],
    )


def per_device(*args):
    length = args[2].shape[1]
    small = length * 11 // 16
    most, prepared = prepare(*args)
    return lax.cond(
        most <= small,
        functools.partial(layer, small),
        functools.partial(layer, length),
        prepared,
        *args,
    )


def solution(mesh):
    split = Mesh(mesh.devices.reshape(mesh.shape["dp"], 2, -1), ("dp", "half", "tp"))
    tensor = ("half", "tp")
    return jax.shard_map(
        per_device,
        mesh=split,
        in_specs=(
            P("dp", None),
            P("dp", None),
            P("dp", None),
            P(),
            P(),
            P(None, tensor),
            P(tensor),
            P(tensor, None),
            P(tensor),
            P(),
            P(),
            P(None, tensor),
            P(tensor),
            P(tensor, None),
            P(tensor),
            P("dp", tensor),
        ),
        out_specs=(
            P("dp", tensor),
            P("dp", tensor),
            P(tensor),
            P(tensor),
            P("dp", tensor),
            P(tensor),
            P(tensor, "dp"),
            P(tensor),
            P(tensor),
            P(tensor),
            P("dp", tensor),
            P(tensor),
            P(tensor, "dp"),
            P(tensor),
        ),
        check_vma=False,
    )
```

```python
import functools

import jax
import jax.numpy as jnp
from jax import lax
from jax.experimental import pallas as pl
from jax.experimental.pallas import tpu as pltpu
from jax.sharding import Mesh, PartitionSpec as P

HD = 64
LAYER = 8
DOCS = 6
EPSILON = 1e-05
MASKED = -1e30
SCALE = HD ** (-0.5)
F32 = jnp.float32
BF = jnp.bfloat16

BQ = 256
BK = 512

BRIEF = pl.CostEstimate(flops=1, bytes_accessed=1, transcendentals=0)

NT = (((1,), (1,)), ((), ()))
TN = (((0,), (0,)), ((), ()))


def mm(left, right):
    return jnp.dot(left, right, preferred_element_type=F32)


def mm_nt(left, right):
    return lax.dot_general(left, right, NT, preferred_element_type=F32)


def mm_tn(left, right):
    return lax.dot_general(left, right, TN, preferred_element_type=F32)


def tie(value, *others):
    return lax.optimization_barrier((value, *others))[0]


def matmul_kernel(dims, at, left_ref, right_ref, *refs):
    out = lax.dot_general(left_ref[...], right_ref[...], dims, preferred_element_type=F32)
    if len(refs) == 2:
        out = out + refs[0][...]
    refs[-1][...] = out.astype(BF)


def brief_mm(left, right, bias=None, transposed=False, half=None):
    rows, depth = left.shape
    at = jnp.zeros((1,), jnp.int32) if half is None else half[None]
    rows = rows if half is None else rows // 2
    columns = right.shape[0] if transposed else right.shape[1]
    size = min(512, columns)
    if transposed:
        right_spec = pl.BlockSpec((size, depth), lambda j, at: (j, 0))
    else:
        right_spec = pl.BlockSpec((depth, size), lambda j, at: (0, j))
    specs = [pl.BlockSpec((rows, depth), lambda j, at: (at[0], 0)), right_spec]
    args = [left, right]
    if bias is not None:
        specs.append(pl.BlockSpec((1, size), lambda j, at: (0, j)))
        args.append(bias[None])
    return pl.pallas_call(
        functools.partial(matmul_kernel, NT if transposed else (((1,), (0,)), ((), ()))),
        grid_spec=pltpu.PrefetchScalarGridSpec(
            num_scalar_prefetch=1,
            grid=(columns // size,),
            in_specs=specs,
            out_specs=pl.BlockSpec((rows, size), lambda j, at: (0, j)),
        ),
        out_shape=jax.ShapeDtypeStruct((rows, columns), BF),
        compiler_params=pltpu.CompilerParams(vmem_limit_bytes=48 * 2**20),
        cost_estimate=BRIEF,
        name="brief_mm",
    )(at, *args)


def pair_mm_kernel(at, one_ref, two_ref, right_ref, bias_ref, kept_ref, sent_ref):
    kept_ref[...] = (mm_nt(one_ref[...], right_ref[...]) + bias_ref[...]).astype(BF)
    sent_ref[...] = (mm_nt(two_ref[...], right_ref[...]) + bias_ref[...]).astype(BF)


def pair_mm(left, right, kept, sent):
    rows, depth = left.shape
    rows = rows // 4
    columns = right.shape[0]
    size = min(512, columns)
    out = pl.BlockSpec((rows, size), lambda j, at: (0, j))
    return pl.pallas_call(
        pair_mm_kernel,
        grid_spec=pltpu.PrefetchScalarGridSpec(
            num_scalar_prefetch=1,
            grid=(columns // size,),
            in_specs=[
                pl.BlockSpec((rows, depth), lambda j, at: (at[0], 0)),
                pl.BlockSpec((rows, depth), lambda j, at: (at[1], 0)),
                pl.BlockSpec((size, depth), lambda j, at: (j, 0)),
                pl.BlockSpec((1, size), lambda j, at: (0, j)),
            ],
            out_specs=[out, out],
        ),
        out_shape=[jax.ShapeDtypeStruct((rows, columns), BF)] * 2,
        compiler_params=pltpu.CompilerParams(vmem_limit_bytes=48 * 2**20),
        cost_estimate=BRIEF,
        name="pair_mm",
    )(jnp.stack((kept, sent)), left, left, right, jnp.zeros((1, columns), F32))


def add_kernel(one_ref, two_ref, out_ref):
    out_ref[...] = (one_ref[...].astype(F32) + two_ref[...].astype(F32)).astype(BF)


def brief_add(one, two):
    rows, width = one.shape
    size = min(512, width)
    tile = pl.BlockSpec((rows, size), lambda j: (0, j))
    return pl.pallas_call(
        add_kernel,
        grid=(width // size,),
        in_specs=[tile, tile],
        out_specs=tile,
        out_shape=jax.ShapeDtypeStruct(one.shape, BF),
        compiler_params=pltpu.CompilerParams(vmem_limit_bytes=40 * 2**20),
        cost_estimate=BRIEF,
        name="brief_add",
    )(one, two)


def far_packed_kernel(count, order, *refs):
    out_ref = refs[-1]
    bias_ref = refs[-2]
    total = mm(refs[0][...], refs[count][...])
    for k in range(1, count):
        total = total + mm(refs[k][...], refs[count + k][...])
    out_ref[...] = (total + bias_ref[...]).astype(BF)


def brief_by_parts(rows, parts, bias):
    count = len(parts)
    depth, columns = parts[0].shape
    size = min(512, rows.shape[0])
    order = jnp.stack([lax.axis_index("dp") ^ k for k in range(count)])
    specs = [
        pl.BlockSpec((size, depth), functools.partial(lambda k, i, order: (i, order[k]), k))
        for k in range(count)
    ]
    specs += [pl.BlockSpec((depth, columns), lambda i, *_: (0, 0))] * count
    specs.append(pl.BlockSpec((1, columns), lambda i, *_: (0, 0)))
    return pl.pallas_call(
        functools.partial(far_packed_kernel, count),
        grid_spec=pltpu.PrefetchScalarGridSpec(
            num_scalar_prefetch=1,
            grid=(rows.shape[0] // size,),
            in_specs=specs,
            out_specs=pl.BlockSpec((size, columns), lambda i, *_: (i, 0)),
        ),
        out_shape=jax.ShapeDtypeStruct((rows.shape[0], columns), BF),
        compiler_params=pltpu.CompilerParams(vmem_limit_bytes=48 * 2**20),
        cost_estimate=BRIEF,
        name="brief_by_parts",
    )(order, *[rows] * count, *parts, bias[None])


def gelu_slope(hidden):
    square = hidden * hidden
    bend = jnp.tanh(0.7978845608 * hidden * (1.0 + 0.044715 * square))
    inner = 0.7978845608 * (1.0 + 3.0 * 0.044715 * square)
    return 0.5 * (1.0 + bend) + 0.5 * hidden * (1.0 - bend * bend) * inner


def unit_back_kernel(grad_ref, weight_ref, hidden_ref, out_ref):
    d_act = mm_nt(grad_ref[...], weight_ref[...])
    out_ref[...] = (d_act * gelu_slope(hidden_ref[...])).astype(BF)


def unit_back(grad, weight, hidden):
    rows, depth = grad.shape
    units = weight.shape[0]
    size = min(512, units)
    tile = pl.BlockSpec((rows, size), lambda j: (0, j))
    return pl.pallas_call(
        unit_back_kernel,
        grid=(units // size,),
        in_specs=[
            pl.BlockSpec((rows, depth), lambda j: (0, 0)),
            pl.BlockSpec((size, depth), lambda j: (j, 0)),
            tile,
        ],
        out_specs=tile,
        out_shape=jax.ShapeDtypeStruct((rows, units), BF),
        compiler_params=pltpu.CompilerParams(vmem_limit_bytes=48 * 2**20),
        cost_estimate=BRIEF,
        name="unit_back",
    )(grad, weight, hidden)


def grad_kernel(pairs, *refs):
    total = sum(mm_tn(refs[2 * i][...], refs[2 * i + 1][...]) for i in range(pairs))
    at = 0
    for out_ref in refs[2 * pairs :]:
        out_ref[...] = total[:, at : at + out_ref.shape[1]].astype(BF)
        at += out_ref.shape[1]


def brief_grad(pairs, widths):
    rows = pairs[0][0].shape[1]
    size = min(256, rows)
    specs = []
    args = []
    for left, right in pairs:
        specs.append(pl.BlockSpec((left.shape[0], size), lambda i: (0, i)))
        specs.append(pl.BlockSpec(right.shape, lambda i: (0, 0)))
        args += [left, right]
    return pl.pallas_call(
        functools.partial(grad_kernel, len(pairs)),
        grid=(rows // size,),
        in_specs=specs,
        out_specs=[pl.BlockSpec((size, width), lambda i: (i, 0)) for width in widths],
        out_shape=[jax.ShapeDtypeStruct((rows, width), BF) for width in widths],
        compiler_params=pltpu.CompilerParams(vmem_limit_bytes=52 * 2**20),
        cost_estimate=BRIEF,
        name="brief_grad",
    )(*args)


def norm_kernel(half, x_ref, gain_ref, shift_ref, out_ref):
    wide = x_ref[...].astype(F32)
    mean = jnp.mean(wide, axis=1, keepdims=True)
    centred = wide - mean
    inv = lax.rsqrt(jnp.mean(centred * centred, axis=1, keepdims=True) + EPSILON)
    out_ref[...] = (centred * inv * gain_ref[...] + shift_ref[...]).astype(BF)


def norm_rows(tokens, half, length, gain, shift):
    width = tokens.shape[1]
    size = 256
    steps = length // size
    vector = pl.BlockSpec((1, width), lambda i, *_: (0, 0))
    return pl.pallas_call(
        norm_kernel,
        grid_spec=pltpu.PrefetchScalarGridSpec(
            num_scalar_prefetch=1,
            grid=(steps,),
            in_specs=[
                pl.BlockSpec((size, width), lambda i, at: (at[0] * steps + i, 0)),
                vector,
                vector,
            ],
            out_specs=pl.BlockSpec((size, width), lambda i, at: (i, 0)),
        ),
        out_shape=jax.ShapeDtypeStruct((length, width), BF),
        compiler_params=pltpu.CompilerParams(vmem_limit_bytes=40 * 2**20),
        cost_estimate=BRIEF,
        name="norm_rows",
    )(half[None], tokens, gain[None], shift[None])


def norm_back_kernel(at, kept_ref, near_ref, far_ref, *refs):
    if len(refs) == 6:
        standard_ref, inv_ref, add_ref, gain_ref, out_ref, sums_ref = refs
        standard = standard_ref[...]
        inv = inv_ref[...]
        add = add_ref[...].astype(F32)
    else:
        x_ref, add_ref, gain_ref, out_ref, sums_ref = refs
        wide = x_ref[...].astype(F32)
        centred = wide - jnp.mean(wide, axis=1, keepdims=True)
        inv = lax.rsqrt(jnp.mean(centred * centred, axis=1, keepdims=True) + EPSILON)
        standard = centred * inv
        add = add_ref[...].astype(F32)
    grad = kept_ref[...].astype(F32) + near_ref[...].astype(F32) + far_ref[...].astype(F32)
    scaled = grad * gain_ref[...]
    moment = jnp.mean(scaled * standard, axis=1, keepdims=True)
    result = add + inv * (scaled - jnp.mean(scaled, axis=1, keepdims=True) - standard * moment)
    out_ref[...] = result.astype(BF)

    @pl.when(pl.program_id(0) == 0)
    def _():
        sums_ref[...] = jnp.zeros_like(sums_ref)

    sums_ref[0:1, :] += jnp.sum(grad * standard, axis=0, keepdims=True)
    sums_ref[1:2, :] += jnp.sum(grad, axis=0, keepdims=True)
    if len(refs) == 6:
        sums_ref[2:3, :] += jnp.sum(result.astype(BF).astype(F32), axis=0, keepdims=True)
        sums_ref[3:4, :] += jnp.sum(add, axis=0, keepdims=True)


def norm_back(kept, mine, near, far, gain, *inputs, token_block=None):
    rows, width = near.shape
    size = rows // 2 if (rows // 2) % 16 == 0 else rows
    steps = rows // size
    if token_block is None:
        token_block = jnp.zeros_like(mine)
    tile = pl.BlockSpec((size, width), lambda i, at: (i, 0))
    specs = [pl.BlockSpec((size, width), lambda i, at: (at[0] * steps + i, 0)), tile, tile]
    if len(inputs) == 3:
        specs += [tile, pl.BlockSpec((size, 1), lambda i, at: (i, 0)), tile]
    else:
        specs += [pl.BlockSpec((size, width), lambda i, at: (at[1] * steps + i, 0)), tile]
    specs.append(pl.BlockSpec((1, width), lambda i, at: (0, 0)))
    return pl.pallas_call(
        norm_back_kernel,
        grid_spec=pltpu.PrefetchScalarGridSpec(
            num_scalar_prefetch=1,
            grid=(steps,),
            in_specs=specs,
            out_specs=[tile, pl.BlockSpec((8, width), lambda i, at: (0, 0))],
        ),
        out_shape=[
            jax.ShapeDtypeStruct((rows, width), BF),
            jax.ShapeDtypeStruct((8, width), F32),
        ],
        compiler_params=pltpu.CompilerParams(vmem_limit_bytes=48 * 2**20),
        cost_estimate=BRIEF,
        name="norm_back",
    )(jnp.stack((mine, token_block)), kept, near, far, *inputs, gain[None])


def spread_rows_kernel(near_ids, far_ids, slot, near_ref, far_ref, out_ref, near_one, far_one):
    @pl.when(pl.program_id(0) == 0)
    def _():
        near_one[...] = (near_ids[...] == slot[...]).astype(BF)
        far_one[...] = (far_ids[...] == slot[...]).astype(BF)

    total = mm_tn(near_one[...], near_ref[...]) + mm_tn(far_one[...], far_ref[...])
    out_ref[...] = total.astype(BF)


def spread_rows(near, far, near_ids, far_ids, slot):
    rows, width = near.shape
    tokens = slot.shape[0]
    size = min(512, width)
    tile = pl.BlockSpec((rows, size), lambda j: (0, j))
    ids = pl.BlockSpec((rows, 1), lambda j: (0, 0))
    return pl.pallas_call(
        spread_rows_kernel,
        grid=(width // size,),
        in_specs=[ids, ids, pl.BlockSpec((1, tokens), lambda j: (0, 0)), tile, tile],
        out_specs=pl.BlockSpec((tokens, size), lambda j: (0, j)),
        out_shape=jax.ShapeDtypeStruct((tokens, width), BF),
        scratch_shapes=[pltpu.VMEM((rows, tokens), BF)] * 2,
        compiler_params=pltpu.CompilerParams(vmem_limit_bytes=40 * 2**20),
        cost_estimate=BRIEF,
        name="spread_rows",
    )(near_ids[:, None], far_ids[:, None], slot[None], near, far)


def row_sums_kernel(*refs):
    refs[-1][...] = sum(jnp.sum(r[...].astype(F32), axis=0, keepdims=True) for r in refs[:-1])


def row_sums(*arrays):
    width = arrays[0].shape[1]
    size = 512 if width % 512 == 0 else width
    return pl.pallas_call(
        row_sums_kernel,
        grid=(width // size,),
        in_specs=[pl.BlockSpec((array.shape[0], size), lambda i: (0, i)) for array in arrays],
        out_specs=pl.BlockSpec((1, size), lambda i: (0, i)),
        out_shape=jax.ShapeDtypeStruct((1, width), F32),
        compiler_params=pltpu.CompilerParams(vmem_limit_bytes=40 * 2**20),
        cost_estimate=BRIEF,
        name="row_sums",
    )(*arrays)[0]


def gather_kernel(x_ref, pos_ref, out_ref):
    wanted = pos_ref[0]
    total = jnp.zeros(out_ref.shape, F32)
    for start in range(0, x_ref.shape[0], BK):
        here = start + lax.broadcasted_iota(jnp.int32, (BK, wanted.shape[1]), 0)
        total = total + mm_tn((here == wanted).astype(BF), x_ref[start : start + BK, :])
    out_ref[...] = total.astype(BF)


def gather_slots(values, positions, capacity, length):
    rows = positions.shape[0]
    width = values.shape[1]
    return pl.pallas_call(
        gather_kernel,
        grid=(rows,),
        in_specs=[
            pl.BlockSpec((length, width), lambda r: (r, 0)),
            pl.BlockSpec((1, 1, capacity), lambda r: (r, 0, 0)),
        ],
        out_specs=pl.BlockSpec((capacity, width), lambda r: (r, 0)),
        out_shape=jax.ShapeDtypeStruct((rows * capacity, width), BF),
        compiler_params=pltpu.CompilerParams(vmem_limit_bytes=40 * 2**20),
        cost_estimate=BRIEF,
        name="gather_slots",
    )(values, positions[:, None, :capacity])


def place_kernel(wide, at, slots_ref, slot_ref, base_ref, *refs):
    out_ref = refs[-1]
    capacity = slots_ref.shape[0]
    size, width = out_ref.shape
    here = lax.broadcasted_iota(jnp.int32, (capacity, size), 0)
    one = (here == slot_ref[0]).astype(BF)
    hit = mm_tn(one, jnp.ones((capacity, width), BF))
    result = jnp.where(hit > 0.5, mm_tn(one, slots_ref[...]), base_ref[...].astype(F32))
    if wide:
        result = result + refs[0][...].astype(F32)
    out_ref[...] = result.astype(out_ref.dtype)


def place_tokens(slot_values, slot, base, column, addend=None):
    rows, length = slot.shape
    width = slot_values.shape[1]
    capacity = slot_values.shape[0] // rows
    size = 512
    steps = length // size
    token_spec = pl.BlockSpec((size, width), lambda r, i, *_: (r * steps + i, 0))
    if base.shape[1] % 128 == 0 and width % 128 == 0:
        base_spec = pl.BlockSpec((size, width), lambda r, i, at: (r * steps + i, at[0]))
    else:
        base = lax.dynamic_slice_in_dim(base, column * width, width, 1)
        base_spec = token_spec
    out_type = BF if addend is None else F32
    extra = [] if addend is None else [addend]
    return pl.pallas_call(
        functools.partial(place_kernel, addend is not None),
        grid_spec=pltpu.PrefetchScalarGridSpec(
            num_scalar_prefetch=1,
            grid=(rows, steps),
            in_specs=[
                pl.BlockSpec((capacity, width), lambda r, i, *_: (r, 0)),
                pl.BlockSpec((1, 1, size), lambda r, i, *_: (r, 0, i)),
                base_spec,
            ]
            + [token_spec] * len(extra),
            out_specs=token_spec,
        ),
        out_shape=jax.ShapeDtypeStruct((rows * length, width), out_type),
        compiler_params=pltpu.CompilerParams(vmem_limit_bytes=40 * 2**20),
        cost_estimate=BRIEF,
        name="place_tokens",
    )(column[None], slot_values, slot[:, None, :], base, *extra)


def finish_kernel(active_ref, base_ref, add_ref, out_ref):
    base = jnp.where(active_ref[...] > 0.0, 0.0, base_ref[...].astype(F32))
    out_ref[...] = add_ref[...].astype(F32) + base


def finish_tokens(active, base, add):
    rows, width = base.shape
    size = 512
    tile = pl.BlockSpec((size, width), lambda i: (i, 0))
    return pl.pallas_call(
        finish_kernel,
        grid=(rows // size,),
        in_specs=[pl.BlockSpec((size, 1), lambda i: (i, 0)), tile, tile],
        out_specs=tile,
        out_shape=jax.ShapeDtypeStruct((rows, width), F32),
        compiler_params=pltpu.CompilerParams(vmem_limit_bytes=32 * 2**20),
        cost_estimate=BRIEF,
        name="finish_tokens",
    )(active, base, add)


def split_heads(pairs, heads):
    lane = lax.broadcasted_iota(jnp.int32, (pairs.shape[0], 128), 1)
    out = []
    for pair in range(heads // 2):
        part = pairs[:, 128 * pair : 128 * pair + 128]
        zero = jnp.zeros_like(part)
        out += [jnp.where(lane < 64, part, zero), jnp.where(lane < 64, zero, part)]
    return out


def merge_heads(parts, block):
    row = lax.broadcasted_iota(jnp.int32, (128, block), 0)
    return [
        jnp.where(row < 64, parts[2 * pair], parts[2 * pair + 1])
        for pair in range(len(parts) // 2)
    ]


def unpack(heads, packed_ref, q_all, k_all, v_all):
    lane = lax.broadcasted_iota(jnp.int32, (packed_ref.shape[0], 128), 1)
    for pair in range(heads // 2):
        lanes = slice(128 * pair, 128 * pair + 128)
        part = [packed_ref[:, 384 * pair + 128 * i : 384 * pair + 128 * i + 128] for i in range(3)]
        q_all[:, lanes] = jnp.where(lane < 64, part[0], part[1])
        keys = jnp.where(lane < 64, part[2], part[0])
        k_all[:, lanes] = pltpu.roll(keys.astype(F32), 64, 1).astype(BF)
        v_all[:, lanes] = jnp.where(lane < 64, part[1], part[2])


def attend_kernel(
    heads,
    first,
    last,
    near,
    packed_ref,
    lo_ref,
    hi_ref,
    o_ref,
    low_ref,
    lse_ref,
    q_ref,
    q_all,
    k_all,
    v_all,
):
    block = pl.program_id(0)

    @pl.when(block == 0)
    def _():
        unpack(heads, packed_ref, q_all, k_all, v_all)

    lo = lo_ref[...]
    hi = hi_ref[...]

    def pick_step(window, total):
        start = pl.multiple_of(window * BK, BK)
        here = start + lax.broadcasted_iota(jnp.int32, (BK, BQ), 0)
        return total + mm_tn((here == hi).astype(BF), q_all[pl.ds(start, BK), :])

    picked = lax.fori_loop(near[block], last[block], pick_step, jnp.zeros(q_ref.shape, F32))
    picked = picked.astype(BF)
    q_ref[...] = picked
    queries = split_heads(picked * jnp.asarray(SCALE, BF), heads)

    def step(key_block, carried):
        start = pl.multiple_of(key_block * BK, BK)
        key_pos = start + lax.broadcasted_iota(jnp.int32, (BK, BQ), 0)
        allowed = (key_pos >= lo) & (key_pos <= hi)
        raw = [
            mm_nt(k_all[pl.ds(start, BK), 128 * (h // 2) : 128 * (h // 2) + 128], queries[h])
            for h in range(heads)
        ]
        out = []
        for h in range(heads):
            values = v_all[pl.ds(start, BK), 128 * (h // 2) : 128 * (h // 2) + 128]
            top, total, mixed = carried[3 * h : 3 * h + 3]
            scores = jnp.where(allowed, raw[h], MASKED)
            new_top = jnp.maximum(top, jnp.max(scores, axis=0, keepdims=True))
            weights = jnp.exp(scores - new_top)
            fade = jnp.exp(top - new_top)
            total = total * fade + jnp.sum(weights, axis=0, keepdims=True)
            mixed = mixed * fade + mm_tn(values, weights.astype(BF))
            out += [new_top, total, mixed]
        return tuple(out)

    init = (
        jnp.full((1, BQ), MASKED, F32),
        jnp.zeros((1, BQ), F32),
        jnp.zeros((128, BQ), F32),
    ) * heads
    done = lax.fori_loop(first[block], last[block], step, init)
    merged = merge_heads([done[3 * h + 2] / done[3 * h + 1] for h in range(heads)], BQ)
    for pair in range(heads // 2):
        part = merged[pair].T
        o_ref[:, 128 * pair : 128 * pair + 128] = part
        low_ref[:, 128 * pair : 128 * pair + 128] = part.astype(BF)
    row = lax.broadcasted_iota(jnp.int32, (8, BQ), 0)
    lse = jnp.zeros((8, BQ), F32)
    for h in range(heads):
        lse = jnp.where(row == h, done[3 * h] + jnp.log(done[3 * h + 1]), lse)
    lse_ref[...] = lse


def attend(packed, lo, hi, bounds):
    count = hi.shape[1]
    length = packed.shape[0]
    width = packed.shape[1] // 3
    heads = width // HD
    row_spec = pl.BlockSpec((1, BQ), lambda i, *_: (0, i))
    block_spec = pl.BlockSpec((BQ, width), lambda i, *_: (i, 0))
    spec = pltpu.PrefetchScalarGridSpec(
        num_scalar_prefetch=3,
        grid=(count // BQ,),
        in_specs=[
            pl.BlockSpec((length, 3 * width), lambda i, *_: (0, 0)),
            row_spec,
            row_spec,
        ],
        out_specs=[
            block_spec,
            block_spec,
            pl.BlockSpec((8, BQ), lambda i, *_: (0, i)),
            block_spec,
        ],
        scratch_shapes=[pltpu.VMEM((length, width), BF)] * 3,
    )
    return pl.pallas_call(
        functools.partial(attend_kernel, heads),
        grid_spec=spec,
        out_shape=[
            jax.ShapeDtypeStruct((count, width), F32),
            jax.ShapeDtypeStruct((count, width), BF),
            jax.ShapeDtypeStruct((8, count), F32),
            jax.ShapeDtypeStruct((count, width), BF),
        ],
        compiler_params=pltpu.CompilerParams(vmem_limit_bytes=48 * 2**20),
        cost_estimate=BRIEF,
        name="attend",
    )(*bounds, packed, lo, hi)


def attend_back_kernel(
    heads,
    first,
    last,
    near,
    packed_ref,
    q_ref,
    g_ref,
    o_ref,
    lse_ref,
    lo_ref,
    hi_ref,
    *refs,
):
    out_ref, q_all, k_all, v_all, dq_sum, dk_sum, dv_sum = refs[-7:]
    count, width = q_ref.shape
    unpack(heads, packed_ref, q_all, k_all, v_all)
    dq_sum[...] = jnp.zeros_like(dq_sum)
    dk_sum[...] = jnp.zeros_like(dk_sum)
    dv_sum[...] = jnp.zeros_like(dv_sum)
    head_of = lax.broadcasted_iota(jnp.int32, (8, width), 1) // HD
    picks = (head_of == lax.broadcasted_iota(jnp.int32, (8, width), 0)).astype(F32)

    def query_step(block, _):
        at = pl.multiple_of(block * BQ, BQ)
        queries = split_heads(q_ref[pl.ds(at, BQ), :] * jnp.asarray(SCALE, BF), heads)
        grad = g_ref[pl.ds(at, BQ), :]
        grads = split_heads(grad, heads)
        lo = lo_ref[:, pl.ds(at, BQ)]
        hi = hi_ref[:, pl.ds(at, BQ)]
        delta = lax.dot_general(
            picks,
            grad.astype(F32) * o_ref[pl.ds(at, BQ), :],
            NT,
            precision=lax.Precision.HIGHEST,
            preferred_element_type=F32,
        )

        def key_step(key_block, carried):
            start = pl.multiple_of(key_block * BK, BK)
            key_pos = start + lax.broadcasted_iota(jnp.int32, (BK, BQ), 0)
            allowed = (key_pos >= lo) & (key_pos <= hi)
            out = []
            for pair in range(heads // 2):
                lanes = slice(128 * pair, 128 * pair + 128)
                keys = k_all[pl.ds(start, BK), lanes]
                values = v_all[pl.ds(start, BK), lanes]
                dk = dk_sum[pl.ds(start, BK), lanes]
                dv = dv_sum[pl.ds(start, BK), lanes]
                for h in (2 * pair, 2 * pair + 1):
                    scores = mm_nt(keys, queries[h])
                    shares = jnp.exp(
                        jnp.where(allowed, scores, MASKED) - lse_ref[h : h + 1, pl.ds(at, BQ)]
                    )
                    d_shares = mm_nt(values, grads[h])
                    d_scores = (shares * (d_shares - delta[h : h + 1, :])).astype(BF)
                    dv = dv + mm(shares.astype(BF), grads[h])
                    dk = dk + mm(d_scores, queries[h])
                    out.append(carried[h] + mm_tn(keys, d_scores))
                dk_sum[pl.ds(start, BK), lanes] = dk
                dv_sum[pl.ds(start, BK), lanes] = dv
            return tuple(out)

        done = lax.fori_loop(
            first[block], last[block], key_step, (jnp.zeros((128, BQ), F32),) * heads
        )
        d_queries = [(part.T * SCALE).astype(BF) for part in merge_heads(done, BQ)]

        def place_step(window, _):
            start = pl.multiple_of(window * BK, BK)
            here = start + lax.broadcasted_iota(jnp.int32, (BK, BQ), 0)
            one = (here == hi).astype(BF)
            for pair in range(heads // 2):
                lanes = slice(128 * pair, 128 * pair + 128)
                dq_sum[pl.ds(start, BK), lanes] += mm(one, d_queries[pair])
            return 0

        lax.fori_loop(near[block], last[block], place_step, 0)
        return 0

    lax.fori_loop(0, count // BQ, query_step, 0)
    lane = lax.broadcasted_iota(jnp.int32, (out_ref.shape[0], 128), 1)
    for pair in range(heads // 2):
        lanes = slice(128 * pair, 128 * pair + 128)
        dq = dq_sum[:, lanes]
        dk = pltpu.roll(dk_sum[:, lanes], 64, 1)
        dv = dv_sum[:, lanes]
        merged = (
            jnp.where(lane < 64, dq, dk),
            jnp.where(lane < 64, dv, dq),
            jnp.where(lane < 64, dk, dv),
        )
        for i, part in enumerate(merged):
            out_ref[:, 384 * pair + 128 * i : 384 * pair + 128 * i + 128] = part.astype(BF)


def attend_back(packed, queries, grads, column, mixed, lse, lo, hi, bounds, sets, joined):
    count, width = queries.shape
    length = packed.shape[0]
    heads = width // HD
    query_spec = pl.BlockSpec((count, width), lambda i, *_: (0, 0))
    grad_spec = pl.BlockSpec((count, width), lambda i, *_: (0, column))
    packed_spec = pl.BlockSpec((length, 3 * width), lambda i, *_: (0, 0))
    row_spec = pl.BlockSpec((1, count), lambda i, *_: (0, 0))
    spec = pltpu.PrefetchScalarGridSpec(
        num_scalar_prefetch=3,
        grid=(1,),
        in_specs=[
            packed_spec,
            query_spec,
            grad_spec,
            query_spec,
            pl.BlockSpec((8, count), lambda i, *_: (0, 0)),
            row_spec,
            row_spec,
        ]
        + [pl.BlockSpec(memory_space=pl.ANY)] * (joined is not None),
        out_specs=pl.BlockSpec((length, 3 * width), lambda i, *_: (0, column)),
        scratch_shapes=[pltpu.VMEM((length, width), BF)] * 3
        + [pltpu.VMEM((length, width), F32)] * 3,
    )
    return pl.pallas_call(
        functools.partial(attend_back_kernel, heads),
        grid_spec=spec,
        out_shape=jax.ShapeDtypeStruct((length, 3 * width * sets), BF),
        input_output_aliases={} if joined is None else {10: 0},
        compiler_params=pltpu.CompilerParams(vmem_limit_bytes=58 * 2**20),
        cost_estimate=BRIEF,
        name="attend_back",
    )(*bounds, packed, queries, grads, mixed, lse, lo, hi, *([] if joined is None else [joined]))


def swap_halves(value):
    return lax.ppermute(value, "half", [(0, 1), (1, 0)])


def swap_by_gather(value):
    rows = value.shape[0]
    pair = lax.all_gather(value, "half", axis=0, tiled=True)
    return lax.dynamic_slice_in_dim(pair, (1 - lax.axis_index("half")) * rows, rows, 0)


def exchange(value, bit, axis="tp"):
    return lax.ppermute(value, axis, [(i, i ^ bit) for i in range(lax.axis_size(axis))])


def gather_near(value):
    bit = 1
    while bit < lax.axis_size("tp") // 2:
        value = jnp.concatenate((value, exchange(value, bit)), axis=0)
        bit *= 2
    return value


def send_top(value):
    return exchange(value, lax.axis_size("tp") // 2)


def fold_parts(value, natural, *beside, bit=None):
    bit = lax.axis_size("tp") // 4 if bit is None else bit
    place = lax.axis_index("tp")
    while True:
        rows = value.shape[0] // 2
        mine = (place // bit) % 2 if natural else jnp.zeros_like(place)
        sent = lax.dynamic_slice_in_dim(value, (1 - mine) * rows, rows, 0) if natural else value[rows:]
        received = exchange(sent.astype(BF), bit)
        received = tie(received, *beside) if beside else received
        if bit == 1:
            return value, mine, received
        value = add_parts(value, mine, received)
        bit //= 2


def add_parts(kept, mine, received):
    rows = received.shape[0]
    kept = lax.dynamic_slice_in_dim(kept, mine * rows, rows, 0)
    return kept.astype(F32) + received.astype(F32)


def fold_tp(value, *beside):
    return add_parts(*fold_parts(value, False, *beside))


def fold_natural(value):
    return add_parts(*fold_parts(value, True))


def natural_halves(value):
    rows = value.shape[0] // 2
    top = lax.axis_index("tp") // (lax.axis_size("tp") // 2)
    return (
        lax.dynamic_slice_in_dim(value, top * rows, rows, 0),
        lax.dynamic_slice_in_dim(value, (1 - top) * rows, rows, 0),
    )


def relative_rows(value):
    count = lax.axis_size("tp")
    size = value.shape[0] // count
    place = lax.axis_index("tp")
    blocks = [
        lax.dynamic_slice_in_dim(value, (place ^ k) * size, size, 0) for k in range(count)
    ]
    middle = count // 2
    return jnp.concatenate(blocks[:middle], axis=0), jnp.concatenate(blocks[middle:], axis=0)


def both(parts):
    return jnp.concatenate(parts, axis=0)


def own_dp_part(weight):
    part = weight.shape[0] // lax.axis_size("dp")
    return lax.dynamic_slice_in_dim(weight, lax.axis_index("dp") * part, part, 0)


def spread_first(part):
    return exchange(part, 1, "dp"), exchange(part, 2, "dp")


def spread_second(part, first):
    count = lax.axis_size("dp")
    one, two = first
    middle = part.shape[0] // 2
    blocks = [(0, 0, part), (1, 0, one), (2, 0, two)]
    blocks.append((3, 0, exchange(two[:middle], 1, "dp")))
    blocks.append((3, middle, exchange(one[middle:], 2, "dp")))
    bit = 4
    while bit < count:
        blocks = blocks + [(k + bit, at, exchange(block, bit, "dp")) for k, at, block in blocks]
        bit *= 2
    return blocks


def whole_parts(blocks):
    parts = {}
    for k, _, block in blocks:
        parts.setdefault(k, []).append(block)
    return [jnp.concatenate(parts[k], axis=0) for k in range(len(parts))]


def assemble(buffer, blocks, row, column):
    member = lax.axis_index("dp")
    size = buffer.shape[0] - row
    part = size // lax.axis_size("dp")
    for k, offset, block in blocks:
        start = row + (member ^ k) * part + offset
        buffer = lax.dynamic_update_slice(buffer, block, (start, column))
    return buffer


def sum_over_dp(grad, dimension):
    return lax.psum_scatter(grad.astype(BF), "dp", scatter_dimension=dimension, tiled=True)


ALL = ("half", "tp")


def running_count(flags):
    rows, length = flags.shape
    chunk = 128
    tiles = flags.reshape(rows, length // chunk, chunk)
    ones = (
        lax.broadcasted_iota(jnp.int32, (chunk, chunk), 0)
        <= lax.broadcasted_iota(jnp.int32, (chunk, chunk), 1)
    ).astype(BF)
    inside = jnp.einsum("rtc,cd->rtd", tiles.astype(BF), ones, preferred_element_type=F32)
    totals = jnp.sum(tiles, axis=2)
    tile_count = length // chunk
    earlier = (
        lax.broadcasted_iota(jnp.int32, (tile_count, tile_count), 0)
        < lax.broadcasted_iota(jnp.int32, (tile_count, tile_count), 1)
    ).astype(F32)
    before = jnp.sum(totals[:, :, None] * earlier[None], axis=1)
    return (inside + before[:, :, None]).reshape(rows, length)


def prepare(
    tokens,
    segment_ids,
    exit_layer,
    norm1_gain,
    norm1_shift,
    w_qkv,
    b_qv,
    w_out,
    b_out,
    norm2_gain,
    norm2_shift,
    w_up,
    b_up,
    w_down,
    b_down,
    cotangent,
):
    half = lax.axis_index("half")
    rows, length = segment_ids.shape
    own_heads = b_qv.shape[0] // (2 * HD)

    far_qkv_part = swap_halves(own_dp_part(w_qkv))
    far_out_part = swap_halves(own_dp_part(w_out))
    far_vectors = swap_halves(jnp.concatenate((b_qv, b_up, b_out, b_down)))

    active = exit_layer > LAYER
    most = jnp.max(jnp.sum(active.astype(F32), axis=1)) * jnp.ones((8, 128), F32)
    bit = 1
    while bit < lax.axis_size("dp"):
        most = jnp.maximum(most, exchange(most, bit, "dp"))
        bit *= 2

    normed1 = norm_rows(
        tokens, half, length, norm1_gain.astype(F32), norm1_shift.astype(F32)
    )
    own_packed = (mm(normed1, w_qkv) + qkv_bias(b_qv)).astype(BF)

    running = running_count(active.astype(F32)).astype(jnp.int32)
    slot = jnp.where(active, running - 1, -1)
    slots = lax.broadcasted_iota(jnp.int32, (1, length, 1), 1)
    positions = jnp.sum((running[:, None, :] <= slots).astype(jnp.int32), axis=2)
    own_positions = lax.dynamic_index_in_dim(positions, half, 0, keepdims=False)
    own_docs = lax.dynamic_index_in_dim(segment_ids, half, 0, keepdims=False)
    doc_numbers = jnp.arange(DOCS, dtype=jnp.int32)[:, None]
    doc_starts = jnp.sum((own_docs[None, :] < doc_numbers).astype(jnp.int32), axis=1, keepdims=True)
    hi = jnp.minimum(own_positions, length - 1)
    lo = jnp.max(jnp.where(doc_starts <= hi[None, :], doc_starts, 0), axis=0)
    prepared = (far_qkv_part, far_out_part, far_vectors, normed1, own_packed)
    prepared += (slot, positions, own_positions, lo, hi)
    return most[0, 0], prepared


def qkv_bias(bias):
    pairs = bias.astype(F32).reshape(-1, 2, HD)
    zero = jnp.zeros_like(pairs[:, 0])
    return jnp.stack((pairs[:, 0], zero, pairs[:, 1]), axis=1).reshape(-1)


def layer(
    capacity,
    prepared,
    tokens,
    segment_ids,
    exit_layer,
    norm1_gain,
    norm1_shift,
    w_qkv,
    b_qv,
    w_out,
    b_out,
    norm2_gain,
    norm2_shift,
    w_up,
    b_up,
    w_down,
    b_down,
    cotangent,
):
    far_qkv_part, far_out_part, far_vectors, normed1, own_packed = prepared[:5]
    slot, positions, own_positions, lo, hi = prepared[5:]
    n_tp = lax.axis_size("tp")
    half = lax.axis_index("half")
    place = lax.axis_index("tp")
    rows, length = segment_ids.shape
    width = tokens.shape[1]
    own_width = cotangent.shape[1]
    device = half * n_tp + place
    own_heads = b_qv.shape[0] // (2 * HD)
    units = w_up.shape[1]
    cap_all = -(-capacity // BQ) * BQ
    cap_part = capacity // n_tp
    part = length // n_tp
    gain1 = norm1_gain.astype(F32)

    lo = lo[:cap_all]
    hi = hi[:cap_all]
    bounds = (lo[::BQ] // BK, hi[BQ - 1 :: BQ] // BK + 1, hi[::BQ] // BK)
    lo = lo[None]
    hi = hi[None]

    size = b_qv.shape[0]
    far_b_qv = far_vectors[:size]
    far_b_up = far_vectors[size : size + units]
    far_b_out = far_vectors[size + units : size + units + own_width]
    far_b_down = far_vectors[size + units + own_width :]

    def share_of_bias(own, far):
        bias = jnp.zeros((width,), F32)
        bias = lax.dynamic_update_slice(bias, own.astype(F32), (device * own_width,))
        other = (1 - half) * n_tp + place
        return lax.dynamic_update_slice(bias, far.astype(F32), (other * own_width,))

    far_qkv_first = spread_first(far_qkv_part)
    far_out = lax.all_gather(far_out_part, "dp", axis=0, tiled=True)
    own_cot = gather_slots(cotangent, positions, capacity, length)
    cot = lax.all_to_all(own_cot, ALL, split_axis=0, concat_axis=1, tiled=True)

    if own_heads % 2:
        far_qkv_blocks = spread_second(far_qkv_part, far_qkv_first)
        far_qkv = assemble(jnp.zeros_like(w_qkv), far_qkv_blocks, 0, 0)
        far_packed = (mm(normed1, far_qkv) + qkv_bias(far_b_qv)).astype(BF)
        packs = [jnp.concatenate((own_packed, far_packed), axis=1)]
        far_up_part = swap_halves(own_dp_part(w_up))
        kept = [attend(packs[0], lo, hi, bounds)]
    else:
        own_kept = attend(own_packed, lo, hi, bounds)
        far_out, far_qkv_first, *own_kept = lax.optimization_barrier(
            (far_out, far_qkv_first, *own_kept)
        )
        far_qkv_blocks = spread_second(far_qkv_part, far_qkv_first)
        far_up_part = swap_by_gather(tie(own_dp_part(w_up), far_out))
        far_packed = brief_by_parts(normed1, whole_parts(far_qkv_blocks), qkv_bias(far_b_qv))
        packs = [own_packed, far_packed]
        kept = [own_kept, attend(far_packed, lo, hi, bounds)]
    far_up_part, cot, head_out = lax.optimization_barrier(
        (far_up_part, cot, jnp.concatenate([item[1] for item in kept], axis=1))
    )
    far_down_part = swap_by_gather(tie(own_dp_part(w_down), far_up_part))
    far_up_first = spread_first(far_up_part)

    out_weight = jnp.concatenate((w_out, far_out), axis=0)
    head_out = head_out[:capacity]
    near_rows, far_rows = natural_halves(head_out)
    out_bias = share_of_bias(b_out, far_b_out)
    far_branch = fold_natural((mm(far_rows, out_weight) + out_bias).astype(BF)).astype(BF)
    near_branch = fold_natural((mm(near_rows, out_weight) + out_bias).astype(BF))
    recv_branch = send_top(far_branch)
    part_positions = lax.dynamic_slice_in_dim(own_positions, place * cap_part, cap_part)
    part_pick = (
        part_positions[:, None] == lax.broadcasted_iota(jnp.int32, (1, length), 1)
    ).astype(BF)
    own_inputs = lax.dynamic_slice_in_dim(tokens, half * length, length, 0)
    part_inputs = mm(tie(part_pick, far_branch), own_inputs).astype(BF)
    qkv_weight = assemble(
        jnp.pad(tie(w_qkv, far_branch), ((0, 0), (0, w_qkv.shape[1]))),
        far_qkv_blocks,
        0,
        w_qkv.shape[1],
    )
    up_weight = jnp.pad(tie(w_up, far_branch), ((0, 0), (0, units)))
    near_d_ffn = gather_near(cot)
    far_up_first, part_inputs = lax.optimization_barrier((far_up_first, part_inputs))
    far_up_blocks = spread_second(far_up_part, far_up_first)
    up_weight = assemble(up_weight, far_up_blocks, 0, units)
    down_weight = jnp.pad(tie(w_down, far_branch), ((0, units), (0, 0)))
    recv_branch, near_branch, up_weight, qkv_weight, down_weight = lax.optimization_barrier(
        (recv_branch, near_branch, up_weight, qkv_weight, down_weight)
    )
    residual = part_inputs.astype(F32) + near_branch + recv_branch.astype(F32)
    mean2 = jnp.mean(residual, axis=1, keepdims=True)
    inv2 = lax.rsqrt(jnp.mean(jnp.square(residual - mean2), axis=1, keepdims=True) + EPSILON)
    standard2 = (residual - mean2) * inv2
    gain2 = norm2_gain.astype(F32)
    part_normed2 = (standard2 * gain2 + norm2_shift.astype(F32)).astype(BF)
    far_down_first = spread_first(far_down_part)
    near_normed2 = gather_near(part_normed2)
    far_normed2 = send_top(part_normed2)
    up_bias = jnp.concatenate((b_up, far_b_up)).astype(F32)

    def forward(part_in):
        hidden = mm(part_in, up_weight) + up_bias
        return jax.nn.gelu(hidden, approximate=True).astype(BF), hidden

    near_act, near_hidden = forward(near_normed2)
    far_normed2, near_act, far_down_first = lax.optimization_barrier(
        (far_normed2, near_act, far_down_first)
    )
    far_cot = send_top(tie(cot, far_normed2))
    far_normed2 = gather_near(far_normed2)
    far_act, far_hidden = forward(far_normed2)
    down_weight = assemble(
        down_weight, spread_second(far_down_part, far_down_first), units, 0
    )
    down_weight, far_act, far_cot = lax.optimization_barrier((down_weight, far_act, far_cot))
    far_d_ffn = gather_near(far_cot)
    far_d_hidden = (mm_nt(far_d_ffn, down_weight) * gelu_slope(far_hidden)).astype(BF)
    down_bias = share_of_bias(b_down, far_b_down)
    far_d_normed2 = mm_nt(far_d_hidden, up_weight).astype(BF)
    far_ffn = (mm(tie(far_act, far_d_normed2), down_weight) + down_bias).astype(BF)
    far_d_normed2 = fold_tp(far_d_normed2, far_ffn).astype(BF)
    recv_d_normed2 = send_top(far_d_normed2)
    (grad_down,) = brief_grad(
        ((tie(near_act, far_d_normed2), near_d_ffn), (far_act, far_d_ffn)), (width,)
    )
    near_d_hidden = unit_back(tie(near_d_ffn, grad_down), down_weight, near_hidden)
    grad_down_sum = sum_over_dp(grad_down.reshape(2, units, width), 2)
    near_d_normed2 = brief_mm(near_d_hidden, up_weight, None, True)
    recv_d_normed2, near_d_normed2, grad_down = lax.optimization_barrier(
        (recv_d_normed2, near_d_normed2, grad_down)
    )
    near_d_normed2 = fold_parts(near_d_normed2, False)

    d_branch_part, sums2 = norm_back(*near_d_normed2, recv_d_normed2, gain2, standard2, inv2, cot)
    far_d_branch = send_top(d_branch_part)
    near_d_branch = gather_near(d_branch_part)
    near_d_heads = brief_mm(near_d_branch, out_weight, None, True)
    near_ffn = brief_mm(tie(near_act, near_d_heads), down_weight, down_bias)
    (grad_up,) = brief_grad(
        ((tie(near_normed2, near_ffn), near_d_hidden), (far_normed2, far_d_hidden)), (2 * units,)
    )
    far_d_branch, grad_up, near_ffn = lax.optimization_barrier((far_d_branch, grad_up, near_ffn))
    far_ffn = fold_tp(tie(far_ffn, far_d_branch)).astype(BF)
    near_ffn = fold_tp(tie(near_ffn, far_d_branch))
    recv_ffn = send_top(far_ffn)
    far_d_branch = gather_near(far_d_branch)
    d_heads = both((near_d_heads, mm_nt(far_d_branch, out_weight).astype(BF)))
    d_heads = jnp.pad(both(relative_rows(d_heads)), ((0, cap_all - capacity), (0, 0)))
    d_heads, grad_down = lax.optimization_barrier((d_heads, grad_down_sum))
    grad_up = sum_over_dp(tie(grad_up, grad_down), 0)
    far_swap_down = swap_halves(grad_down[1])

    def back(at, joined):
        item = kept[at]
        return attend_back(
            packs[at], item[3], d_heads, at, item[0], item[2], lo, hi, bounds, len(packs), joined
        )

    d_pack = back(0, None)
    head_rows = relative_rows(head_out)
    (grad_out,) = brief_grad(
        ((tie(head_rows[0], d_pack), near_d_branch), (head_rows[1], far_d_branch)), (width,)
    )
    d_pack, grad_out = lax.optimization_barrier((d_pack, grad_out))
    if len(packs) == 2:
        d_pack = back(1, d_pack)
    d_pack, recv_ffn, far_swap_down = lax.optimization_barrier((d_pack, recv_ffn, far_swap_down))
    out_part = (residual + near_ffn + recv_ffn.astype(F32)).astype(BF)
    out_slots = lax.all_to_all(out_part, ALL, split_axis=1, concat_axis=0, tiled=True)
    d_pack = tie(d_pack, out_part)
    d_pack, grad_up = lax.optimization_barrier((d_pack, grad_up))
    far_up = grad_up[:, units:]
    d_pack = tie(d_pack, far_up)
    far_swap_up = swap_halves(far_up)
    grad_out = sum_over_dp(tie(grad_out, grad_up), 1)
    top = place // (n_tp // 2)
    bit = n_tp // 4
    mine = (place // bit) % 2
    kept, sent = pair_mm(d_pack, qkv_weight, 2 * (1 - top) + mine, 2 * (1 - top) + 1 - mine)
    far_d_normed1 = brief_add(kept, exchange(sent, bit))
    if bit > 1:
        far_d_normed1 = add_parts(*fold_parts(far_d_normed1, True, bit=bit // 2)).astype(BF)
    recv_d_normed1 = send_top(far_d_normed1)
    near_pair = pair_mm(
        tie(d_pack, far_d_normed1), qkv_weight, 2 * top + mine, 2 * top + 1 - mine
    )
    near_received = exchange(near_pair[1], bit)
    near_d_normed1 = near_pair[0]
    qkv_width = w_qkv.shape[1]
    d_hidden_sums = row_sums(tie(near_d_hidden, far_d_normed1), far_d_hidden)
    d_pack_sums = row_sums(tie(d_pack, far_d_normed1))
    far_unit_sums = swap_halves(
        jnp.concatenate((d_pack_sums[qkv_width:], d_hidden_sums[units:]))
    )
    (raw_grad_qkv,) = brief_grad(((tie(normed1, near_d_normed1), d_pack),), (2 * qkv_width,))
    place_ids = jnp.arange(cap_part, dtype=jnp.int32)
    slot_ids = [(place ^ k) * cap_part + place_ids for k in range(n_tp)]
    part_slot = lax.dynamic_slice(slot, (half, place * part), (1, part))[0]
    d_residual_rows = spread_rows(
        tie(near_d_branch, raw_grad_qkv),
        far_d_branch,
        jnp.concatenate(slot_ids[: n_tp // 2]),
        jnp.concatenate(slot_ids[n_tp // 2 :]),
        part_slot,
    )
    (
        recv_d_normed1,
        raw_grad_qkv,
        grad_out,
        out_slots,
        far_swap_up,
        far_unit_sums,
        d_residual_rows,
    ) = lax.optimization_barrier(
        (
            recv_d_normed1,
            raw_grad_qkv,
            grad_out,
            out_slots,
            far_swap_up,
            far_unit_sums,
            d_residual_rows,
        )
    )
    grad_qkv = sum_over_dp(raw_grad_qkv, 0)
    out_rows = w_out.shape[0]
    far_swap_out = swap_halves(grad_out[out_rows:])
    near_d_normed1 = (near_d_normed1, jnp.zeros_like(place), near_received)
    if bit > 1:
        near_d_normed1 = fold_parts(add_parts(*near_d_normed1).astype(BF), True, bit=bit // 2)

    d_norm1_part, sums1 = norm_back(
        *near_d_normed1,
        recv_d_normed1,
        gain1,
        tokens,
        d_residual_rows,
        token_block=half * n_tp + place,
    )
    d_norm1_part, far_swap_out = lax.optimization_barrier((d_norm1_part, far_swap_out))
    features = jnp.concatenate((sums1[:2], sums2[:4])).astype(BF)
    features = jnp.pad(features, ((0, 16 - features.shape[0]), (0, 0)))
    spread = lax.all_to_all(
        jnp.concatenate((d_norm1_part, features), axis=0),
        ALL,
        split_axis=1,
        concat_axis=0,
        tiled=True,
    )
    result = place_tokens(out_slots, tie(slot, d_norm1_part), tokens, device)
    spread, result = lax.optimization_barrier((spread, result))
    spread = spread.reshape(-1, part + 16, own_width)
    d_norm1_tokens = spread[:, :part].reshape(-1, own_width)
    feature_sums = jnp.sum(spread[:, part : part + 6].astype(F32), axis=0).reshape(-1)
    own_unit_sums = jnp.concatenate((d_pack_sums[:qkv_width], d_hidden_sums[:units]))
    summed = lax.psum(jnp.concatenate((feature_sums, own_unit_sums + far_unit_sums)), "dp")
    grad_qkv = tie(grad_qkv, d_norm1_tokens)
    far_swap_qkv = swap_halves(grad_qkv[:, qkv_width:])
    active = (slot >= 0).astype(F32).reshape(rows * length, 1)
    d_inputs = finish_tokens(active, cotangent, d_norm1_tokens)

    def join(own, far):
        return own.astype(F32) + far.astype(F32)

    grad_down = join(grad_down[0], far_swap_down)
    grad_up = join(grad_up[:, :units], far_swap_up)
    grad_out = join(grad_out[:out_rows], far_swap_out)
    grad_qkv = join(grad_qkv[:, :qkv_width], far_swap_qkv)

    feature_sums = summed[: 6 * own_width].reshape(6, own_width)
    unit_sums = summed[6 * own_width :]
    d_biases = unit_sums[:qkv_width].reshape(own_heads, 3, HD)
    d_biases = jnp.stack((d_biases[:, 0], d_biases[:, 2]), axis=1).reshape(-1)
    return (
        result,
        d_inputs,
        feature_sums[0],
        feature_sums[1],
        grad_qkv,
        d_biases,
        grad_out,
        feature_sums[4],
        feature_sums[2],
        feature_sums[3],
        grad_up,
        unit_sums[qkv_width:],
        grad_down,
        feature_sums[5],
    )


def per_device(*args):
    length = args[2].shape[1]
    small = length * 11 // 16
    most, prepared = prepare(*args)
    return lax.cond(
        most <= small,
        functools.partial(layer, small),
        functools.partial(layer, length),
        prepared,
        *args,
    )


def solution(mesh):
    split = Mesh(mesh.devices.reshape(mesh.shape["dp"], 2, -1), ("dp", "half", "tp"))
    tensor = ("half", "tp")
    return jax.shard_map(
        per_device,
        mesh=split,
        in_specs=(
            P("dp", None),
            P("dp", None),
            P("dp", None),
            P(),
            P(),
            P(None, tensor),
            P(tensor),
            P(tensor, None),
            P(tensor),
            P(),
            P(),
            P(None, tensor),
            P(tensor),
            P(tensor, None),
            P(tensor),
            P("dp", tensor),
        ),
        out_specs=(
            P("dp", tensor),
            P("dp", tensor),
            P(tensor),
            P(tensor),
            P("dp", tensor),
            P(tensor),
            P(tensor, "dp"),
            P(tensor),
            P(tensor),
            P(tensor),
            P("dp", tensor),
            P(tensor),
            P(tensor, "dp"),
            P(tensor),
        ),
        check_vma=False,
    )
```
